128 devices in a mesh: tm: 16 (over z_lo, y, core), space: 8 (over z_hi, x).
Axes of the slice: x: 4, y: 4, z: 4 (z_hi: 2, z_lo: 2; z = z_hi * 2 + z_lo), core: 2. Of those that a mesh axis runs over, the one named last changes fastest.
Arguments:
- initial_states: float32 [16, 1024, 2048], P('tm', 'space'), may hold values from -6 to 6
- sources: float32 [16, 1024, 2048], P('tm', 'space'), may hold values from -4 to 4
- tile_class: int32 [8, 16], replicated, may hold values from 0 to 7
- coeff_sets: float32 [3, 8], replicated, may hold values from -0.5 to 0.5, as said below
- coarse_maps: float32 [16, 512, 512], P('tm'), may hold values from -1 to 1
Outputs:
- final_states: float32 [16, 1024, 2048], P('tm', 'space')
The draws below stay inside these ranges and needn't reach their ends.
Inputs may be any that keep to these rules, and one draw needn't show every extreme that they name: `tile_class`: which of the 8 coefficient sets each 128 x 128 tile of cells uses. `coeff_sets`: row 0 holds positive diffusivities up to 0.12, rows 1 and 2 velocities along columns and along rows.
All inputs are finite; a program needn't handle non-finite values.
Results may differ from the reference program's by a relative error of at most 0.00019.
Values sent between devices are 32-bit elements; how exact they have to be, the bound alone decides.
No kernel may reach another device: no remote copies, remote signals or barrier semaphores. Data moves between devices by JAX's collectives and lax.ppermute only.
A program may use at most 64 MiB of HBM per device.

```python
import math
import jax
import jax.numpy as jnp
from jax import lax

NCOL = 2048
TILE = 128
BLK = 64
STEPS = 8
ITERS = 2
WINDOWS = 16
NROW = 1024
TROWS = 8
TCOLS = 16
COARSE = 512


def draw_coeff_sets(key, part):
    key = jax.random.fold_in(key, 5)
    first_key = jax.random.fold_in(key, 0)
    third_key = jax.random.fold_in(key, 2)
    diffusivity = jnp.exp(jax.random.uniform(first_key, (8,), minval=math.log(0.02), maxval=math.log(0.12)))
    speeds = jax.random.uniform(third_key, (2, 8), minval=-0.5, maxval=0.5)
    return jnp.concatenate([diffusivity[None, :], speeds], axis=0).astype(jnp.float32)


def draw_coarse_maps(key, part):
    key = jax.random.fold_in(key, 11)
    diag_key, other_key = jax.random.split(key, 2)
    diagonal = jax.random.uniform(diag_key, (WINDOWS, COARSE), minval=0.75, maxval=0.95)
    others = jax.random.normal(other_key, (WINDOWS, COARSE, COARSE)) * (0.35 / math.sqrt(COARSE))
    identity = jnp.eye(COARSE, dtype=jnp.float32)
    combined = others + diagonal[:, :, None] * identity[None, :, :]
    return jnp.clip(combined, -1.0, 1.0).astype(jnp.float32)


def touch_ends(drawn, stream_key, low, top_value):
    place = [jax.random.randint(jax.random.fold_in(stream_key, axis), (), 0, length) for axis, length in enumerate(drawn.shape)]
    widest = drawn.shape.index(max(drawn.shape))
    neighbour = place[:widest] + [(place[widest] + 1) % drawn.shape[widest]] + place[widest + 1:]
    return drawn.at[tuple(place)].set(low).at[tuple(neighbour)].set(top_value)


def level_of(rng, extent, cuts, low, top_value):
    def one(position, blocks):
        steps = jax.random.uniform(jax.random.fold_in(jax.random.fold_in(rng, 6), position), (blocks,), jnp.float32, low / len(cuts), top_value / len(cuts))
        return jnp.repeat(jnp.exp(steps), extent[position] // blocks).reshape((-1,) + (1,) * (len(extent) - position - 1))

    loudness = one(*cuts[0])
    for cut in cuts[1:]:
        loudness = loudness * one(*cut)
    return loudness


def gaussian(key, shape, deviation, limit, pieces=(), kind=jnp.bfloat16):
    values = jax.random.normal(key, shape, jnp.float32) * deviation
    if len(pieces) > 0:
        values = level_of(key, shape, pieces, -0.22, 0.18) * values
    return jnp.clip(values, min=-limit, max=limit).astype(kind)


def setup_inputs(seed: int = 0) -> dict:
    seeds = jax.random.split(jax.random.key(seed), 6)
    initial_states = gaussian(seeds[0], (WINDOWS, NROW, NCOL), 1.0, 6.0, ((0, 16), (1, 8)), jnp.float32)
    sources = gaussian(seeds[1], (WINDOWS, NROW, NCOL), 0.3, 4.0, ((0, 16), (1, 8)), jnp.float32)
    tile_class = touch_ends(jax.random.randint(seeds[2], (TROWS, TCOLS), 0, 8), jax.random.fold_in(seeds[2], 1), 0, 7).astype(jnp.int32)
    coeff_sets = draw_coeff_sets(jax.random.fold_in(seeds[5], 71), 0)
    coarse_maps = draw_coarse_maps(jax.random.fold_in(seeds[5], 71), 0)
    return {"initial_states": initial_states, "sources": sources, "tile_class": tile_class, "coeff_sets": coeff_sets, "coarse_maps": coarse_maps}


step_size = 0.6


def advance(center, upper_rows, lower_rows, diffusivity, speed_cols, speed_rows, source):
    left_cells = jnp.roll(center, 1, axis=1)
    right_cells = jnp.roll(center, -1, axis=1)
    laplace = upper_rows + lower_rows + left_cells + right_cells - 4.0 * center
    transport = (jnp.maximum(speed_cols, 0.0) * (center - left_cells)
                 + jnp.minimum(speed_cols, 0.0) * (right_cells - center)
                 + jnp.maximum(speed_rows, 0.0) * (center - upper_rows)
                 + jnp.minimum(speed_rows, 0.0) * (lower_rows - center))
    return center + step_size * (diffusivity * laplace - transport + source)


def reference(initial_states, sources, tile_class, coeff_sets, coarse_maps):
    classes = jnp.repeat(jnp.repeat(tile_class, TILE, axis=0), TILE, axis=1)
    diffusivity = coeff_sets[0][classes]
    speed_cols = coeff_sets[1][classes]
    speed_rows = coeff_sets[2][classes]

    def sweep(paired):
        start_state, source = paired

        def one_step(turn_index, carried):
            return advance(carried, jnp.roll(carried, 1, axis=0), jnp.roll(carried, -1, axis=0),
                           diffusivity, speed_cols, speed_rows, source)

        return lax.fori_loop(0, STEPS, one_step, start_state)

    states = initial_states
    for outer_index in range(ITERS):
        finished = lax.map(sweep, (states, sources))
        previous = jnp.roll(finished, 1, axis=0)
        defect = previous - states
        coarse_defect = defect.reshape(WINDOWS, NROW // BLK, BLK, NCOL // BLK, BLK).mean(axis=(2, 4)).reshape(WINDOWS, COARSE)

        def link_step(turn_index, carried):
            mapped = jnp.einsum("nij,nj->ni", coarse_maps, coarse_defect + carried,
                                precision=lax.Precision.HIGHEST)
            return jnp.roll(mapped, 1, axis=0)

        correction = lax.fori_loop(0, 2 * WINDOWS, link_step, jnp.zeros((WINDOWS, COARSE), jnp.float32))
        blocks = correction.reshape(WINDOWS, NROW // BLK, 1, NCOL // BLK, 1)
        spread = jnp.broadcast_to(blocks, (WINDOWS, NROW // BLK, BLK, NCOL // BLK, BLK)).reshape(WINDOWS, NROW, NCOL)
        states = previous + spread
    return states
```

```python
import functools

import jax
import jax.numpy as jnp
from jax import lax
from jax.experimental import pallas as pl
from jax.experimental.pallas import tpu as pltpu
from jax.sharding import PartitionSpec as P

TILE = 128
BLK = 64
STEPS = 8
ROWS = 128
COLS = 2048
COARSE = 512
HALF = COARSE // 2
TILES = COLS // TILE
EXT = ROWS + 2 * STEPS
LINES = EXT // 8
LOCAL = 64
WIDTH = COARSE + TILE
STEP = 0.6

HIGHEST = lax.Precision.HIGHEST
ANY = pl.BlockSpec(memory_space=pl.ANY)
SMEM = pl.BlockSpec(memory_space=pltpu.SMEM)
VMEM = pl.BlockSpec(memory_space=pltpu.VMEM)


def place(device):
    tm, space = divmod(device, 8)
    z_lo, rest = divmod(tm, 8)
    y, core = divmod(rest, 2)
    z_hi, x = divmod(space, 4)
    return x, y, 2 * z_hi + z_lo, core


def device_at(x, y, z, core):
    x, y, z, core = x % 4, y % 4, z % 4, core % 2
    return ((z % 2) * 8 + y * 2 + core) * 8 + (z // 2) * 4 + x


def moved(value, route):
    pairs = [(i, device_at(*route(*place(i)))) for i in range(128)]
    return lax.ppermute(value, ("tm", "space"), pairs)


def shifted(value, windows, strips=0):
    pairs = [
        (tm * 8 + sp, (tm + windows) % 16 * 8 + (sp + strips) % 8)
        for tm in range(16)
        for sp in range(8)
    ]
    return lax.ppermute(value, ("tm", "space"), pairs)


def iota(shape, axis):
    return lax.broadcasted_iota(jnp.int32, shape, axis)


def packed_means(sums):
    lane = iota((32, TILE), 1)
    row = iota((32, TILE), 0)
    low = jnp.sum(jnp.where(lane < BLK, sums, 0.0), axis=1, keepdims=True)
    high = jnp.sum(jnp.where(lane < BLK, 0.0, sums), axis=1, keepdims=True)
    slot = lane & (LOCAL - 1)
    spread = jnp.where(slot == 2 * row, low, 0.0) + jnp.where(slot == 2 * row + 1, high, 0.0)
    return jnp.sum(spread, axis=0, keepdims=True) * (1.0 / (BLK * BLK))


def means_kernel(u_ref, out_ref, sums_ref):
    for k in range(TILES):
        cols = slice(k * TILE, (k + 1) * TILE)
        for br in range(2):
            part = u_ref[br * BLK : (br + 1) * BLK, cols]
            sums_ref[br * TILES + k : br * TILES + k + 1, :] = jnp.sum(part, axis=0, keepdims=True)
    out_ref[...] = packed_means(sums_ref[...])


def block_means(u):
    return pl.pallas_call(
        means_kernel,
        out_shape=jax.ShapeDtypeStruct((1, TILE), jnp.float32),
        in_specs=[VMEM],
        out_specs=VMEM,
        scratch_shapes=[pltpu.VMEM((32, TILE), jnp.float32)],
        compiler_params=pltpu.CompilerParams(vmem_limit_bytes=16 << 20),
    )(u)


def pair_kernel(ids_ref, own_ref, other_ref, half_ref, columns_ref, late, early, sems):
    strip, core = ids_ref[0], ids_ref[1]

    def both(first, second):
        a = pltpu.make_async_copy(first, late, sems.at[0])
        b = pltpu.make_async_copy(second, early, sems.at[1])
        a.start()
        b.start()
        a.wait()
        b.wait()

    @pl.when(core == 1)
    def _():
        both(own_ref, other_ref)

    @pl.when(core == 0)
    def _():
        both(other_ref, own_ref)

    rows = late[pl.ds(pl.multiple_of(core * HALF, HALF), HALF), :]
    half_ref[...] = jnp.dot(rows, early[...], precision=HIGHEST, preferred_element_type=jnp.float32)
    pick = (iota((LOCAL, COARSE), 1) == iota((LOCAL, COARSE), 0) + strip * LOCAL).astype(jnp.float32)
    contract = (((1,), (1,)), ((), ()))
    taken = lax.dot_general(pick, early[...], contract, precision=HIGHEST, preferred_element_type=jnp.float32)
    taken = jnp.where(core == 1, pick, taken)
    columns_ref[...] = lax.dot_general(
        taken, late[...], contract, precision=HIGHEST, preferred_element_type=jnp.float32
    )


def pair_product(ids, own, other):
    return pl.pallas_call(
        pair_kernel,
        out_shape=(
            jax.ShapeDtypeStruct((HALF, COARSE), jnp.float32),
            jax.ShapeDtypeStruct((LOCAL, COARSE), jnp.float32),
        ),
        in_specs=[SMEM, ANY, ANY],
        out_specs=(VMEM, VMEM),
        scratch_shapes=[
            pltpu.VMEM((COARSE, COARSE), jnp.float32),
            pltpu.VMEM((COARSE, COARSE), jnp.float32),
            pltpu.SemaphoreType.DMA((2,)),
        ],
        compiler_params=pltpu.CompilerParams(vmem_limit_bytes=24 << 20),
    )(ids, own, other)


def fine_kernel(corrected, ids_ref, class_ref, sets_ref, *refs):
    if corrected:
        c_ref, *refs = refs
    (u_ref, up_ref, down_ref, f_ref, f_up_ref, f_down_ref) = refs[:6]
    fin_ref, means_ref = refs[6:8]
    u_ext, f_ext, first, second, force, coef, sums_ref, sems = refs[8:]
    strip = ids_ref[0]
    copies = []
    for n, (source, target, start, rows) in enumerate(
        (
            (u_ref, u_ext, STEPS, ROWS),
            (f_ref, f_ext, STEPS, ROWS),
            (up_ref, u_ext, 0, STEPS),
            (down_ref, u_ext, STEPS + ROWS, STEPS),
            (f_up_ref, f_ext, 0, STEPS),
            (f_down_ref, f_ext, STEPS + ROWS, STEPS),
        )
    ):
        for k in range(TILES):
            cols = pl.ds(k * TILE, TILE)
            copy = pltpu.make_async_copy(source.at[:, cols], target.at[k, pl.ds(start, rows)], sems.at[n, k])
            copy.start()
            copies.append(copy)

    sub = iota((8, TILE), 0)
    lane = iota((8, TILE), 1)
    strips = (lax.rem(strip + 7, 8), strip, lax.rem(strip + 1, 8))

    def weights(row, k):
        label = class_ref[row, k]
        spread, along_cols, along_rows = sets_ref[0, label], sets_ref[1, label], sets_ref[2, label]
        left = STEP * (spread + jnp.maximum(along_cols, 0.0))
        right = STEP * (spread - jnp.minimum(along_cols, 0.0))
        above = STEP * (spread + jnp.maximum(along_rows, 0.0))
        below = STEP * (spread - jnp.minimum(along_rows, 0.0))
        return 1.0 - (left + right + above + below), left, right, above, below

    for k in range(TILES):
        upper, inner, lower = (weights(row, k) for row in strips)
        for w in range(5):
            whole = jnp.full((8, TILE), inner[w], jnp.float32)
            coef[k, w] = jnp.where(sub == 0, upper[w], whole)
            coef[k, 5 + w] = whole
            coef[k, 10 + w] = jnp.where(sub == 7, lower[w], whole)

    for copy in copies:
        copy.wait()

    for k in range(TILES):
        if corrected:
            added = []
            for line in range(4):
                block_row = lax.rem(2 * strip + 15 + line, 16)
                added.append(
                    jnp.where(
                        lane < BLK,
                        c_ref[0, block_row * 32 + 2 * k],
                        c_ref[0, block_row * 32 + 2 * k + 1],
                    )
                )
        for i in range(LINES):
            value = u_ext[k, pl.ds(i, 8, stride=LINES), :]
            if corrected:
                row = sub * LINES + i
                addend = jnp.where(row < STEPS + BLK, added[1], added[2])
                addend = jnp.where(row < STEPS, added[0], addend)
                addend = jnp.where(row >= STEPS + ROWS, added[3], addend)
                value = value + addend
            first[k, pl.ds(i * 8, 8), :] = value
            force[k, pl.ds(i * 8, 8), :] = STEP * f_ext[k, pl.ds(i, 8, stride=LINES), :]

    def tile_step(old, new, k):
        before = lax.rem(k + TILES - 1, TILES)
        after = lax.rem(k + 1, TILES)
        line = [old[k, pl.ds(i * 8, 8), :] for i in range(LINES)]
        top = pltpu.roll(line[-1], 1, 0)
        bottom = pltpu.roll(line[0], 7, 0)
        for i in range(LINES):
            kind = 0 if i < STEPS else (1 if i < LINES - STEPS else 2)
            centre, w_left, w_right, w_above, w_below = (coef[k, 5 * kind + w] for w in range(5))
            rows = pl.ds(i * 8, 8)
            left = pltpu.roll(jnp.where(lane == TILE - 1, old[before, rows, :], line[i]), 1, 1)
            right = pltpu.roll(jnp.where(lane == 0, old[after, rows, :], line[i]), TILE - 1, 1)
            above = line[i - 1] if i else top
            below = line[i + 1] if i + 1 < LINES else bottom
            new[k, rows, :] = (
                (centre * line[i] + force[k, rows, :])
                + (w_left * left + w_right * right)
                + (w_above * above + w_below * below)
            )

    def two_steps(_, carry):
        def there(k, carry):
            tile_step(first, second, k)
            return carry

        def back(k, carry):
            tile_step(second, first, k)
            return carry

        lax.fori_loop(0, TILES, there, 0)
        lax.fori_loop(0, TILES, back, 0)
        return carry

    lax.fori_loop(0, STEPS // 2, two_steps, 0)

    results = []
    for k in range(TILES):
        for i in range(LINES):
            u_ext[k, pl.ds(i, 8, stride=LINES), :] = first[k, pl.ds(i * 8, 8), :]
        cols = pl.ds(k * TILE, TILE)
        result = pltpu.make_async_copy(u_ext.at[k, pl.ds(STEPS, ROWS)], fin_ref.at[:, cols], sems.at[0, k])
        result.start()
        results.append(result)
        for br in range(2):
            part = u_ext[k, STEPS + br * BLK : STEPS + (br + 1) * BLK, :]
            sums_ref[br * TILES + k : br * TILES + k + 1, :] = jnp.sum(part, axis=0, keepdims=True)
    means_ref[...] = packed_means(sums_ref[...])
    for result in results:
        result.wait()


def fine_sweep(ids, tile_class, coeff_sets, state, sources, correction=None):
    corrected = correction is not None
    field = pltpu.VMEM((TILES, EXT, TILE), jnp.float32)
    return pl.pallas_call(
        functools.partial(fine_kernel, corrected),
        out_shape=(
            jax.ShapeDtypeStruct((ROWS, COLS), jnp.float32),
            jax.ShapeDtypeStruct((1, TILE), jnp.float32),
        ),
        in_specs=[SMEM, SMEM, SMEM] + [SMEM] * corrected + [ANY] * 6,
        out_specs=(ANY, VMEM),
        scratch_shapes=[
            field,
            field,
            field,
            field,
            field,
            pltpu.VMEM((TILES, 15, 8, TILE), jnp.float32),
            pltpu.VMEM((32, TILE), jnp.float32),
            pltpu.SemaphoreType.DMA((6, TILES)),
        ],
        compiler_params=pltpu.CompilerParams(vmem_limit_bytes=32 << 20),
    )(ids, tile_class, coeff_sets, *([correction] * corrected), *state, *sources)


def message_kernel(ids_ref, means_ref, base_ref, columns_ref, out_ref):
    defect = means_ref[...] - base_ref[...]
    lane = iota((1, TILE), 1)
    pushed = jnp.dot(
        jnp.broadcast_to(defect, (8, TILE))[:, :LOCAL],
        columns_ref[...],
        precision=HIGHEST,
        preferred_element_type=jnp.float32,
    )
    odd = lax.rem(ids_ref[0], 2)
    raw = jnp.where((lane >= LOCAL) == (odd == 1), defect, 0.0)
    raw = jnp.broadcast_to(raw, (8, TILE))
    for n in range(16):
        out_ref[n * 8 : (n + 1) * 8, 0:COARSE] = pushed
        out_ref[n * 8 : (n + 1) * 8, COARSE:WIDTH] = raw


def message(ids, means, base, columns):
    return pl.pallas_call(
        message_kernel,
        out_shape=jax.ShapeDtypeStruct((128, WIDTH), jnp.float32),
        in_specs=[SMEM, VMEM, VMEM, VMEM],
        out_specs=VMEM,
        compiler_params=pltpu.CompilerParams(vmem_limit_bytes=16 << 20),
    )(ids, means, base, columns)


def chain_kernel(ids_ref, got_ref, other_ref, *refs):
    halves = refs[:16]
    out_ref = refs[16]
    maps, early, sems = refs[17:]
    strip, core, chip, y = ids_ref[0], ids_ref[1], ids_ref[2], ids_ref[3]

    def fetch(slot, which):
        mine, theirs = halves[2 * which], halves[2 * which + 1]
        for part, (source, at) in enumerate(((mine, core), (theirs, 1 - core))):
            rows = pl.ds(pl.multiple_of(at * HALF, HALF), HALF)
            pltpu.make_async_copy(source, maps.at[slot, rows], sems.at[slot, part]).start()

    def landed(slot):
        for part in range(2):
            rows = pl.ds(0, HALF)
            pltpu.make_async_copy(halves[0], maps.at[slot, rows], sems.at[slot, part]).wait()

    for ahead in range(1, 4):
        wraps = y + ahead >= 4

        @pl.when(wraps)
        def _():
            fetch(ahead, 4 + ahead)

        @pl.when(jnp.logical_not(wraps))
        def _():
            fetch(ahead, ahead)

    fetch(4, 4)
    for ahead in range(1, 4):
        wraps = y + ahead >= 4

        @pl.when(wraps)
        def _():
            fetch(4 + ahead, ahead)

        @pl.when(jnp.logical_not(wraps))
        def _():
            fetch(4 + ahead, 4 + ahead)

    fetch(0, 0)
    last = pltpu.make_async_copy(other_ref, early, sems.at[8, 0])
    last.start()

    diagonal = iota((TILE, TILE), 0) == iota((TILE, TILE), 1)

    def into_row(column):
        pieces = [
            jnp.sum(jnp.where(diagonal, column[q * TILE : (q + 1) * TILE], 0.0), axis=0, keepdims=True)
            for q in range(4)
        ]
        return jnp.concatenate(pieces, axis=1)

    def applied(matrix, vector):
        return into_row(jnp.sum(matrix * vector, axis=1, keepdims=True))

    def group(window):
        start = pl.multiple_of(lax.rem(window + 16, 16) * 8, 8)
        return jnp.sum(got_ref[pl.ds(start, 8), 0:COARSE], axis=0, keepdims=True)

    def pushed(step):
        at = 2 * lax.rem(chip + step, 8)
        return group(at - 1) + group(at)

    value = jnp.where(core == 1, group(2 * chip), pushed(0))

    def arriving(step, value):
        landed(step)
        return applied(maps[step], value) + pushed(step)

    value = lax.fori_loop(1, 8, arriving, value)
    landed(0)

    def again(step, value):
        return applied(maps[step], value) + pushed(step)

    value = lax.fori_loop(0, 8, again, value)
    last.wait()
    raw = got_ref[pl.ds(pl.multiple_of(lax.rem(2 * chip + 15, 16) * 8, 8), 8), COARSE:WIDTH]
    defect = jnp.concatenate([raw[2 * q : 2 * q + 1] + raw[2 * q + 1 : 2 * q + 2] for q in range(4)], axis=1)
    out_ref[...] = jnp.where(core == 1, applied(early[...], value + defect), value)


def chain(ids, got, other, halves):
    return pl.pallas_call(
        chain_kernel,
        out_shape=jax.ShapeDtypeStruct((1, COARSE), jnp.float32),
        in_specs=[SMEM, VMEM] + [ANY] * 17,
        out_specs=VMEM,
        scratch_shapes=[
            pltpu.VMEM((8, COARSE, COARSE), jnp.float32),
            pltpu.VMEM((COARSE, COARSE), jnp.float32),
            pltpu.SemaphoreType.DMA((9, 2)),
        ],
        compiler_params=pltpu.CompilerParams(vmem_limit_bytes=32 << 20),
    )(ids, got, other, *halves)


def finish_kernel(ids_ref, c_ref, u_ref, out_ref):
    strip = ids_ref[0]
    lane = iota((8, TILE), 1)
    for k in range(TILES):
        cols = slice(k * TILE, (k + 1) * TILE)
        for br in range(2):
            at = (2 * strip + br) * 32 + 2 * k
            added = jnp.where(lane < BLK, c_ref[0, at], c_ref[0, at + 1])
            for n in range(BLK // 8):
                rows = slice(br * BLK + n * 8, br * BLK + (n + 1) * 8)
                out_ref[rows, cols] = u_ref[rows, cols] + added


def finish(ids, correction, previous):
    return pl.pallas_call(
        finish_kernel,
        out_shape=jax.ShapeDtypeStruct((ROWS, COLS), jnp.float32),
        in_specs=[SMEM, SMEM, VMEM],
        out_specs=VMEM,
        compiler_params=pltpu.CompilerParams(vmem_limit_bytes=16 << 20),
    )(ids, correction, previous)


def exchanged(block):
    return lax.all_to_all(block, ("tm", "space"), 0, 0, tiled=True)


def swapped(value):
    return moved(value, lambda x, y, z, core: (x, y, z, 1 - core))


def across(value):
    return moved(value, lambda x, y, z, core: (x, y, z + 1 - 2 * core, core))


def per_device(initial_states, sources, tile_class, coeff_sets, coarse_maps):
    state, source, own_map = initial_states[0], sources[0], coarse_maps[0]
    window = lax.axis_index("tm").astype(jnp.int32)
    strip = lax.axis_index("space").astype(jnp.int32)
    ids = jnp.stack([strip, window % 2, window // 2, (window // 2) % 4])

    other_map = swapped(own_map)
    edges_last = jnp.concatenate([state[-STEPS:], source[-STEPS:]], axis=0)
    edges_first = jnp.concatenate([state[:STEPS], source[:STEPS]], axis=0)
    upper = shifted(edges_last, 0, 1)
    lower = shifted(edges_first, 0, -1)
    start_means = shifted(block_means(state), -1)

    half, columns = pair_product(ids, own_map, other_map)
    below = moved(half, lambda x, y, z, core: (x, y + 1, z, core))
    above = moved(half, lambda x, y, z, core: (x, y - 1, z, core))
    opposite = across(half)
    columns = shifted(columns, -1)

    source_parts = (source, upper[STEPS:], lower[STEPS:])
    finished, means = fine_sweep(
        ids, tile_class, coeff_sets, (state, upper[:STEPS], lower[:STEPS]), source_parts
    )
    previous = shifted(finished, 1)
    previous_up = shifted(finished[-STEPS:], 1, 1)
    previous_down = shifted(finished[:STEPS], 1, -1)

    second = moved(above, lambda x, y, z, core: (x, y - 1, z, core))
    far_second = moved(above, lambda x, y, z, core: (x, y - 1, z + 1 - 2 * core, core))
    far_below = across(below)
    far_above = across(above)

    got = exchanged(message(ids, means, start_means, columns))

    mine = [half, above, second, below, opposite, far_above, far_second, far_below]
    halves = []
    for part in mine:
        halves += [part, swapped(part)]
    correction = chain(ids, got, other_map, halves)

    local = lax.dynamic_slice(correction, (0, strip * LOCAL), (1, LOCAL))
    base = means + shifted(jnp.concatenate([local, local], axis=1), -1)
    finished, means = fine_sweep(
        ids, tile_class, coeff_sets, (previous, previous_up, previous_down), source_parts, correction
    )
    previous = shifted(finished, 1)
    got = exchanged(message(ids, means, base, columns))
    correction = chain(ids, got, other_map, halves)
    return finish(ids, correction, previous)[None]


def solution(mesh):
    placed = (P("tm", "space", None), P("tm", "space", None), P(), P(), P("tm", None, None))
    return jax.shard_map(
        per_device, mesh=mesh, in_specs=placed, out_specs=P("tm", "space", None), check_vma=False
    )
```

```python
import functools

import jax
import jax.numpy as jnp
from jax import lax
from jax.experimental import pallas as pl
from jax.experimental.pallas import tpu as pltpu
from jax.sharding import PartitionSpec as P

TILE = 128
BLK = 64
STEPS = 8
ROWS = 128
COLS = 2048
COARSE = 512
HALF = COARSE // 2
TILES = COLS // TILE
LOCAL = 64
PIECES = 5
STEP = 0.6

HIGHEST = lax.Precision.HIGHEST
HBM = pl.BlockSpec(memory_space=pltpu.HBM)
SMEM = pl.BlockSpec(memory_space=pltpu.SMEM)
VMEM = pl.BlockSpec(memory_space=pltpu.VMEM)


def place(device):
    tm, space = divmod(device, 8)
    z_lo, rest = divmod(tm, 8)
    y, core = divmod(rest, 2)
    z_hi, x = divmod(space, 4)
    return x, y, 2 * z_hi + z_lo, core


def device_at(x, y, z, core):
    x, y, z, core = x % 4, y % 4, z % 4, core % 2
    return ((z % 2) * 8 + y * 2 + core) * 8 + (z // 2) * 4 + x


def moved(value, route):
    pairs = [(i, device_at(*route(*place(i)))) for i in range(128)]
    return lax.ppermute(value, ("tm", "space"), pairs)


def shifted(value, windows, strips=0):
    pairs = [
        (tm * 8 + sp, (tm + windows) % 16 * 8 + (sp + strips) % 8)
        for tm in range(16)
        for sp in range(8)
    ]
    return lax.ppermute(value, ("tm", "space"), pairs)


def iota(shape, axis):
    return lax.broadcasted_iota(jnp.int32, shape, axis)


def packed_means(sums):
    lane = iota((32, TILE), 1)
    row = iota((32, TILE), 0)
    low = jnp.sum(jnp.where(lane < BLK, sums, 0.0), axis=1, keepdims=True)
    high = jnp.sum(jnp.where(lane < BLK, 0.0, sums), axis=1, keepdims=True)
    slot = lane & (LOCAL - 1)
    spread = jnp.where(slot == 2 * row, low, 0.0) + jnp.where(slot == 2 * row + 1, high, 0.0)
    return jnp.sum(spread, axis=0, keepdims=True) * (1.0 / (BLK * BLK))


def pair_kernel(ids_ref, own_ref, other_ref, u_ref, q_ref, half_ref, columns_ref, late, early, u, sums_ref, sems):
    strip, core = ids_ref[0], ids_ref[1]
    state = pltpu.make_async_copy(u_ref, u, sems.at[2])

    def both(first, second):
        a = pltpu.make_async_copy(first, late, sems.at[0])
        b = pltpu.make_async_copy(second, early, sems.at[1])
        a.start()
        b.start()
        state.start()
        a.wait()
        b.wait()

    @pl.when(core == 1)
    def _():
        both(own_ref, other_ref)

    @pl.when(core == 0)
    def _():
        both(other_ref, own_ref)

    def split(value):
        big = value.astype(jnp.bfloat16)
        return big, (value - big.astype(jnp.float32)).astype(jnp.bfloat16)

    def times(a, b):
        return jnp.dot(a, b, preferred_element_type=jnp.float32)

    early_big, early_small = split(early[...])
    for part in range(2):
        rows = slice(part * HALF, (part + 1) * HALF)
        big, small = split(late[rows, :])
        q_ref[rows, :] = times(big, early_big) + (times(big, early_small) + times(small, early_big))
    half_ref[...] = q_ref[pl.ds(pl.multiple_of(core * HALF, HALF), HALF), :]
    cols = pl.ds(pl.multiple_of(strip // 2 * TILE, TILE), TILE)
    wide = jnp.where(core == 1, late[:, cols], q_ref[:, cols])
    turned = jnp.transpose(wide)
    columns_ref[0:LOCAL, :] = jnp.where(lax.rem(strip, 2) == 1, turned[LOCAL:], turned[:LOCAL])
    state.wait()
    for k in range(TILES):
        cols = slice(k * TILE, (k + 1) * TILE)
        for br in range(2):
            part = u[br * BLK : (br + 1) * BLK, cols]
            sums_ref[br * TILES + k : br * TILES + k + 1, :] = jnp.sum(part, axis=0, keepdims=True)
    columns_ref[LOCAL:, :] = jnp.zeros((8, COARSE), jnp.float32)
    columns_ref[LOCAL:, 0:TILE] = jnp.broadcast_to(packed_means(sums_ref[...]), (8, TILE))


def pair_product(ids, own, other, state):
    square = pltpu.VMEM((COARSE, COARSE), jnp.float32)
    return pl.pallas_call(
        pair_kernel,
        out_shape=(
            jax.ShapeDtypeStruct((COARSE, COARSE), jnp.float32),
            jax.ShapeDtypeStruct((HALF, COARSE), jnp.float32),
            jax.ShapeDtypeStruct((LOCAL + 8, COARSE), jnp.float32),
        ),
        in_specs=[SMEM, HBM, HBM, HBM],
        out_specs=(VMEM, VMEM, VMEM),
        scratch_shapes=[
            square,
            square,
            pltpu.VMEM((ROWS, COLS), jnp.float32),
            pltpu.VMEM((32, TILE), jnp.float32),
            pltpu.SemaphoreType.DMA((3,)),
        ],
        compiler_params=pltpu.CompilerParams(vmem_limit_bytes=24 << 20),
    )(ids, own, other, state)


def fine_kernel(halo, corrected, ids_ref, class_ref, sets_ref, *refs):
    if corrected:
        c_ref, *refs = refs
        (u_ref, up_ref, f_ref, down_ref), refs = refs[:4], refs[4:]
    else:
        (up_ref, u_ref, f_ref, down_ref), refs = refs[:4], refs[4:]
    fin_ref, means_ref = refs[:2]
    u_ext, f_ext, first, second, force, coef, sums_ref, sems = refs[2:]
    ext = ROWS + 2 * halo
    lines = ext // 8
    wide = 2 * STEPS
    strip = ids_ref[0]
    if corrected:
        parts = ((u_ref, 0, ext, u_ext, 0),)
    else:
        parts = (
            (u_ref, 0, ROWS, u_ext, halo),
            (up_ref, wide - halo, halo, u_ext, 0),
            (down_ref, 0, halo, u_ext, halo + ROWS),
        )
    parts += (
        (f_ref, 0, ROWS, f_ext, halo),
        (up_ref, 2 * wide - halo, halo, f_ext, 0),
        (down_ref, wide, halo, f_ext, halo + ROWS),
    )
    copies = []
    for k in range(TILES):
        cols = pl.ds(k * TILE, TILE)
        copies.append([])
        for n, (source, at, rows, target, to) in enumerate(parts):
            copy = pltpu.make_async_copy(source.at[pl.ds(at, rows), cols], target.at[k, pl.ds(to, rows)], sems.at[n, k])
            copy.start()
            copies[k].append(copy)

    sub = iota((8, TILE), 0)
    lane = iota((8, TILE), 1)
    strips = (lax.rem(strip + 7, 8), strip, lax.rem(strip + 1, 8))

    def weights(row, k):
        label = class_ref[row, k]
        spread, along_cols, along_rows = sets_ref[0, label], sets_ref[1, label], sets_ref[2, label]
        left = STEP * (spread + jnp.maximum(along_cols, 0.0))
        right = STEP * (spread - jnp.minimum(along_cols, 0.0))
        above = STEP * (spread + jnp.maximum(along_rows, 0.0))
        below = STEP * (spread - jnp.minimum(along_rows, 0.0))
        return 1.0 - (left + right + above + below), left, right, above, below

    kinds = []
    for i in range(lines):
        kind = (i < halo, i >= lines - halo)
        if kind not in kinds:
            kinds.append(kind)
    for k in range(TILES):
        upper, inner, lower = (weights(row, k) for row in strips)
        for n, (top, bottom) in enumerate(kinds):
            for w in range(5):
                value = jnp.full((8, TILE), inner[w], jnp.float32)
                if top:
                    value = jnp.where(sub == 0, upper[w], value)
                if bottom:
                    value = jnp.where(sub == 7, lower[w], value)
                coef[k, 5 * n + w] = value

    for k in range(TILES):
        for copy in copies[k]:
            copy.wait()
        if corrected:
            added = []
            for line in range(4):
                at = lax.rem(2 * strip + 15 + line, 16) * 32 + 2 * k
                added.append(jnp.where(lane < BLK, c_ref[0, at], c_ref[0, at + 1]))
        for i in range(lines):
            value = u_ext[k, pl.ds(i, 8, stride=lines), :]
            if corrected:
                row = sub * lines + i
                addend = jnp.where(row < halo + BLK, added[1], added[2])
                if i < halo:
                    addend = jnp.where(sub == 0, added[0], addend)
                if i >= lines - halo:
                    addend = jnp.where(sub == 7, added[3], addend)
                value = value + addend
            first[k, pl.ds(i * 8, 8), :] = value
            force[k, pl.ds(i * 8, 8), :] = STEP * f_ext[k, pl.ds(i, 8, stride=lines), :]

    def tile_step(old, new, k):
        before = lax.rem(k + TILES - 1, TILES)
        after = lax.rem(k + 1, TILES)
        line = [old[k, pl.ds(i * 8, 8), :] for i in range(lines)]
        top = pltpu.roll(line[-1], 1, 0)
        bottom = pltpu.roll(line[0], 7, 0)
        for i in range(lines):
            kind = kinds.index((i < halo, i >= lines - halo))
            centre, w_left, w_right, w_above, w_below = (coef[k, 5 * kind + w] for w in range(5))
            rows = pl.ds(i * 8, 8)
            left = pltpu.roll(jnp.where(lane == TILE - 1, old[before, rows, :], line[i]), 1, 1)
            right = pltpu.roll(jnp.where(lane == 0, old[after, rows, :], line[i]), TILE - 1, 1)
            above = line[i - 1] if i else top
            below = line[i + 1] if i + 1 < lines else bottom
            new[k, rows, :] = (
                (centre * line[i] + force[k, rows, :])
                + (w_left * left + w_right * right)
                + (w_above * above + w_below * below)
            )

    def two_steps(_, carry):
        def there(k, carry):
            tile_step(first, second, k)
            return carry

        def back(k, carry):
            tile_step(second, first, k)
            return carry

        lax.fori_loop(0, TILES, there, 0, unroll=8)
        lax.fori_loop(0, TILES, back, 0, unroll=8)
        return carry

    lax.fori_loop(0, STEPS // 2, two_steps, 0)

    kept = ext - 2 * STEPS
    results = []
    for k in range(TILES):
        for i in range(lines):
            u_ext[k, pl.ds(i, 8, stride=lines), :] = first[k, pl.ds(i * 8, 8), :]
        cols = pl.ds(k * TILE, TILE)
        result = pltpu.make_async_copy(u_ext.at[k, pl.ds(STEPS, kept)], fin_ref.at[:, cols], sems.at[0, k])
        result.start()
        results.append(result)
        for br in range(2):
            part = u_ext[k, halo + br * BLK : halo + (br + 1) * BLK, :]
            sums_ref[br * TILES + k : br * TILES + k + 1, :] = jnp.sum(part, axis=0, keepdims=True)
    means_ref[...] = packed_means(sums_ref[...])
    for result in results:
        result.wait()


def fine_sweep(ids, tile_class, coeff_sets, fields, correction=None):
    corrected = correction is not None
    halo = STEPS if corrected else 2 * STEPS
    ext = ROWS + 2 * halo
    field = pltpu.VMEM((TILES, ext, TILE), jnp.float32)
    return pl.pallas_call(
        functools.partial(fine_kernel, halo, corrected),
        out_shape=(
            jax.ShapeDtypeStruct((ext - 2 * STEPS, COLS), jnp.float32),
            jax.ShapeDtypeStruct((1, TILE), jnp.float32),
        ),
        in_specs=[SMEM, SMEM, SMEM] + [SMEM] * corrected + [HBM] * 4,
        out_specs=(HBM, VMEM),
        scratch_shapes=[
            field,
            field,
            field,
            field,
            field,
            pltpu.VMEM((TILES, 15, 8, TILE), jnp.float32),
            pltpu.VMEM((32, TILE), jnp.float32),
            pltpu.SemaphoreType.DMA((6, TILES)),
        ],
        compiler_params=pltpu.CompilerParams(vmem_limit_bytes=32 << 20),
    )(ids, tile_class, coeff_sets, *([correction] * corrected), *fields)


def message_kernel(ids_ref, means_ref, base_ref, columns_ref, out_ref, block):
    defect = means_ref[...] - base_ref[...]
    lane = iota((1, TILE), 1)
    pushed = jnp.dot(
        jnp.broadcast_to(defect, (8, TILE))[:, :LOCAL],
        columns_ref[0:LOCAL, :],
        precision=HIGHEST,
        preferred_element_type=jnp.float32,
    )
    odd = lax.rem(ids_ref[0], 2)
    raw = jnp.where((lane >= LOCAL) == (odd == 1), defect, 0.0)
    pieces = [pushed[0:1, q * TILE : (q + 1) * TILE] for q in range(4)] + [raw]
    for n in range(8):
        for q in range(PIECES):
            block[n * PIECES + q : n * PIECES + q + 1, :] = pieces[q]
    for n in range(16):
        out_ref[n * 8 * PIECES : (n + 1) * 8 * PIECES, :] = block[...]


def message(ids, means, base, columns):
    return pl.pallas_call(
        message_kernel,
        out_shape=jax.ShapeDtypeStruct((128 * PIECES, TILE), jnp.float32),
        in_specs=[SMEM, VMEM, VMEM, VMEM],
        out_specs=VMEM,
        scratch_shapes=[pltpu.VMEM((8 * PIECES, TILE), jnp.float32)],
        compiler_params=pltpu.CompilerParams(vmem_limit_bytes=16 << 20),
    )(ids, means, base, columns)


def chain_kernel(last, ids_ref, got_ref, other_ref, *refs):
    whole, refs = refs[:5], refs[5:]
    halved, refs = refs[:6], refs[6:]
    if last:
        u_ref, refs = refs[0], refs[1:]
    out_ref, refs = refs[0], refs[1:]
    if not last:
        local_ref, refs = refs[0], refs[1:]
    maps, early, sems, *refs = refs
    strip, core, chip, y = ids_ref[0], ids_ref[1], ids_ref[2], ids_ref[3]

    def fetch_whole(slot, source):
        for part in range(2):
            rows = pl.ds(part * HALF, HALF)
            pltpu.make_async_copy(source.at[rows], maps.at[slot, rows], sems.at[slot, part]).start()

    def fetch_halves(slot, which):
        for part, at in ((0, core), (1, 1 - core)):
            rows = pl.ds(pl.multiple_of(at * HALF, HALF), HALF)
            pltpu.make_async_copy(halved[2 * which + part], maps.at[slot, rows], sems.at[slot, part]).start()

    def fetch_turned(slot, pair, below):
        mine, theirs = pair
        own = (core == 0) == below

        @pl.when(own)
        def _():
            fetch_whole(slot, mine)

        @pl.when(jnp.logical_not(own))
        def _():
            fetch_whole(slot, theirs)

    def fetch_near(slot, ahead):
        if ahead == 2:
            fetch_halves(slot, 0)
        else:
            fetch_turned(slot, whole[0:2], ahead == 3)

    def fetch_far(slot, ahead):
        if ahead in (0, 2):
            fetch_halves(slot, 2 if ahead else 1)
        else:
            fetch_turned(slot, whole[2:4], ahead == 3)

    def landed(slot):
        for part in range(2):
            rows = pl.ds(0, HALF)
            pltpu.make_async_copy(other_ref.at[rows], maps.at[slot, rows], sems.at[slot, part]).wait()

    for half in range(2):
        if half == 1:
            fetch_far(4, 0)
        for ahead in range(1, 4):
            wraps = y + ahead >= 4

            @pl.when(wraps == (half == 0))
            def _():
                fetch_far(4 * half + ahead, ahead)

            @pl.when(wraps != (half == 0))
            def _():
                fetch_near(4 * half + ahead, ahead)

    fetch_whole(0, whole[4])
    final = pltpu.make_async_copy(other_ref, early, sems.at[8, 0])
    final.start()
    if last:
        u, sem = refs
        state = pltpu.make_async_copy(u_ref, u, sem)
        state.start()

    diagonal = iota((TILE, TILE), 0) == iota((TILE, TILE), 1)

    def applied(matrix, vector):
        row = jnp.concatenate(vector, axis=1)
        column = jnp.sum(matrix * row, axis=1, keepdims=True)
        return [
            jnp.sum(jnp.where(diagonal, column[q * TILE : (q + 1) * TILE], 0.0), axis=0, keepdims=True)
            for q in range(4)
        ]

    def group(window):
        start = lax.rem(window + 16, 16) * (8 * PIECES)
        return [
            jnp.sum(got_ref[pl.ds(start + q, 8, stride=PIECES), :], axis=0, keepdims=True) for q in range(4)
        ]

    def add(a, b):
        return [p + q for p, q in zip(a, b, strict=True)]

    def pushed(step):
        at = 2 * lax.rem(chip + step, 8)
        return add(group(at - 1), group(at))

    value = [jnp.where(core == 1, p, q) for p, q in zip(group(2 * chip), pushed(0), strict=True)]

    def arriving(step, value):
        landed(step)
        return add(applied(maps[step], value), pushed(step))

    value = lax.fori_loop(1, 8, arriving, value)
    landed(0)

    def again(step, value):
        return add(applied(maps[step], value), pushed(step))

    value = lax.fori_loop(0, 8, again, value)
    final.wait()
    start = lax.rem(2 * chip + 15, 16) * (8 * PIECES) + 4
    raw = got_ref[pl.ds(start, 8, stride=PIECES), :]
    defect = [raw[2 * q : 2 * q + 1] + raw[2 * q + 1 : 2 * q + 2] for q in range(4)]
    value = [
        jnp.where(core == 1, p, q) for p, q in zip(applied(early[...], add(value, defect)), value, strict=True)
    ]
    if not last:
        out_ref[...] = jnp.concatenate(value, axis=1)
    lane = iota((8, TILE), 1)
    piece = value[3]
    for q in range(3):
        piece = jnp.where(strip // 2 == q, value[q], piece)
    piece = jnp.broadcast_to(piece, (8, TILE))
    odd = lax.rem(strip, 2)
    if not last:
        here = jnp.where((lane < LOCAL) == (odd == 0), piece, pltpu.roll(piece, LOCAL, 1))
        local_ref[...] = here[0:1]
        return
    state.wait()
    outs = []
    for k in range(TILES):
        cols = slice(k * TILE, (k + 1) * TILE)
        for br in range(2):
            at = odd * LOCAL + br * 32 + 2 * k
            added = jnp.take_along_axis(piece, at + jnp.where(lane < BLK, 0, 1), axis=1)
            for n in range(BLK // 8):
                rows = slice(br * BLK + n * 8, br * BLK + (n + 1) * 8)
                u[rows, cols] = u[rows, cols] + added
        if k % 4 == 3:
            cols = pl.ds((k - 3) * TILE, 4 * TILE)
            copy = pltpu.make_async_copy(u.at[:, cols], out_ref.at[:, cols], sems.at[k // 4, 0])
            copy.start()
            outs.append(copy)
    for copy in outs:
        copy.wait()


def chain(ids, got, other, whole, halved, previous=None):
    last = previous is not None
    if last:
        out_shape, out_specs = jax.ShapeDtypeStruct((ROWS, COLS), jnp.float32), HBM
    else:
        out_shape = (
            jax.ShapeDtypeStruct((1, COARSE), jnp.float32),
            jax.ShapeDtypeStruct((1, TILE), jnp.float32),
        )
        out_specs = (VMEM, VMEM)
    return pl.pallas_call(
        functools.partial(chain_kernel, last),
        out_shape=out_shape,
        in_specs=[SMEM, VMEM] + [HBM] * (12 + last),
        out_specs=out_specs,
        scratch_shapes=[
            pltpu.VMEM((8, COARSE, COARSE), jnp.float32),
            pltpu.VMEM((COARSE, COARSE), jnp.float32),
            pltpu.SemaphoreType.DMA((9, 2)),
        ]
        + [pltpu.VMEM((ROWS, COLS), jnp.float32), pltpu.SemaphoreType.DMA] * last,
        compiler_params=pltpu.CompilerParams(vmem_limit_bytes=32 << 20),
    )(ids, got, other, *whole, *halved, *([previous] * last))


def exchanged(block):
    block = block.reshape(128, 1, PIECES * TILE)
    return lax.all_to_all(block, ("tm", "space"), 0, 0, tiled=True).reshape(128 * PIECES, TILE)


def swapped(value):
    return moved(value, lambda x, y, z, core: (x, y, z, 1 - core))


def across(value):
    return moved(value, lambda x, y, z, core: (x, y, z + 1 - 2 * core, core))


def along(value, dz=0):
    return moved(value, lambda x, y, z, core: (x, y + 1 - 2 * core, z + dz * (1 - 2 * core), core))


def per_device(initial_states, sources, tile_class, coeff_sets, coarse_maps):
    state, source, own_map = initial_states[0], sources[0], coarse_maps[0]
    window = lax.axis_index("tm").astype(jnp.int32)
    strip = lax.axis_index("space").astype(jnp.int32)
    core = window % 2
    ids = jnp.stack([strip, core, window // 2, (window // 2) % 4])
    wide = 2 * STEPS

    other_map = swapped(own_map)
    upper = shifted(jnp.concatenate([state[-wide:], source[-wide:]], axis=0), 0, 1)
    lower = shifted(jnp.concatenate([state[:wide], source[:wide]], axis=0), 0, -1)

    product, half, columns = pair_product(ids, own_map, other_map, state)
    near = along(product)
    far_same = across(half)
    columns = shifted(columns, -1)

    finished, means = fine_sweep(ids, tile_class, coeff_sets, (upper, state, source, lower))
    previous = shifted(finished, 1)

    near_half = lax.dynamic_slice(near, (core * HALF, 0), (HALF, COARSE))
    far = across(near)
    near_second = along(near_half)
    far_second = along(near_half, 1)

    got = exchanged(message(ids, means, columns[LOCAL : LOCAL + 1, :TILE], columns))

    whole = [near, swapped(near), far, swapped(far), product]
    halved = []
    for part in (near_second, far_same, far_second):
        halved += [part, swapped(part)]
    correction, local = chain(ids, got, other_map, whole, halved)

    base = means + shifted(local, -1)
    finished, means = fine_sweep(ids, tile_class, coeff_sets, (previous, upper, source, lower), correction)
    previous = shifted(finished, 1)
    got = exchanged(message(ids, means, base, columns))
    return chain(ids, got, other_map, whole, halved, previous)[None]


def solution(mesh):
    placed = (P("tm", "space", None), P("tm", "space", None), P(), P(), P("tm", None, None))
    return jax.shard_map(
        per_device, mesh=mesh, in_specs=placed, out_specs=P("tm", "space", None), check_vma=False
    )
```

```python
import functools

import jax
import jax.numpy as jnp
from jax import lax
from jax.experimental import pallas as pl
from jax.experimental.pallas import tpu as pltpu
from jax.sharding import PartitionSpec as P

TILE = 128
BLK = 64
STEPS = 8
ROWS = 128
COLS = 2048
COARSE = 512
HALF = COARSE // 2
TILES = COLS // TILE
LOCAL = 64
PIECES = 5
STEP = 0.6

HIGHEST = lax.Precision.HIGHEST
HBM = pl.BlockSpec(memory_space=pltpu.HBM)
SMEM = pl.BlockSpec(memory_space=pltpu.SMEM)
VMEM = pl.BlockSpec(memory_space=pltpu.VMEM)


def place(device):
    tm, space = divmod(device, 8)
    z_lo, rest = divmod(tm, 8)
    y, core = divmod(rest, 2)
    z_hi, x = divmod(space, 4)
    return x, y, 2 * z_hi + z_lo, core


def device_at(x, y, z, core):
    x, y, z, core = x % 4, y % 4, z % 4, core % 2
    return ((z % 2) * 8 + y * 2 + core) * 8 + (z // 2) * 4 + x


def moved(value, route):
    pairs = [(i, device_at(*route(*place(i)))) for i in range(128)]
    return lax.ppermute(value, ("tm", "space"), pairs)


def shifted(value, windows, strips=0):
    pairs = [
        (tm * 8 + sp, (tm + windows) % 16 * 8 + (sp + strips) % 8)
        for tm in range(16)
        for sp in range(8)
    ]
    return lax.ppermute(value, ("tm", "space"), pairs)


def cost(micros):
    return pl.CostEstimate(flops=0, transcendentals=0, bytes_accessed=int(micros * 3.6e6))


def in_hbm(*values):
    return [pltpu.with_memory_space_constraint(value, pltpu.HBM) for value in values]


def iota(shape, axis):
    return lax.broadcasted_iota(jnp.int32, shape, axis)


def packed_means(sums):
    lane = iota((32, TILE), 1)
    row = iota((32, TILE), 0)
    low = jnp.sum(jnp.where(lane < BLK, sums, 0.0), axis=1, keepdims=True)
    high = jnp.sum(jnp.where(lane < BLK, 0.0, sums), axis=1, keepdims=True)
    slot = lane & (LOCAL - 1)
    spread = jnp.where(slot == 2 * row, low, 0.0) + jnp.where(slot == 2 * row + 1, high, 0.0)
    return jnp.sum(spread, axis=0, keepdims=True) * (1.0 / (BLK * BLK))


def pair_kernel(ids_ref, own_ref, other_ref, u_ref, q_ref, half_ref, columns_ref, late, early, u, sums_ref, sems):
    strip, core = ids_ref[0], ids_ref[1]
    state = pltpu.make_async_copy(u_ref, u, sems.at[2])

    def both(first, second):
        a = pltpu.make_async_copy(first, late, sems.at[0])
        b = pltpu.make_async_copy(second, early, sems.at[1])
        a.start()
        b.start()
        state.start()
        a.wait()
        b.wait()

    @pl.when(core == 1)
    def _():
        both(own_ref, other_ref)

    @pl.when(core == 0)
    def _():
        both(other_ref, own_ref)

    def split(value):
        big = value.astype(jnp.bfloat16)
        return big, (value - big.astype(jnp.float32)).astype(jnp.bfloat16)

    def times(a, b):
        return jnp.dot(a, b, preferred_element_type=jnp.float32)

    early_big, early_small = split(early[...])
    for part in range(2):
        rows = slice(part * HALF, (part + 1) * HALF)
        big, small = split(late[rows, :])
        q_ref[rows, :] = times(big, early_big) + (times(big, early_small) + times(small, early_big))
    half_ref[...] = q_ref[pl.ds(pl.multiple_of(core * HALF, HALF), HALF), :]
    cols = pl.ds(pl.multiple_of(strip // 2 * TILE, TILE), TILE)
    wide = jnp.where(core == 1, late[:, cols], q_ref[:, cols])
    turned = jnp.transpose(wide)
    columns_ref[0:LOCAL, :] = jnp.where(lax.rem(strip, 2) == 1, turned[LOCAL:], turned[:LOCAL])
    state.wait()
    for k in range(TILES):
        cols = slice(k * TILE, (k + 1) * TILE)
        for br in range(2):
            part = u[br * BLK : (br + 1) * BLK, cols]
            sums_ref[br * TILES + k : br * TILES + k + 1, :] = jnp.sum(part, axis=0, keepdims=True)
    columns_ref[LOCAL:, :] = jnp.zeros((8, COARSE), jnp.float32)
    columns_ref[LOCAL:, 0:TILE] = jnp.broadcast_to(packed_means(sums_ref[...]), (8, TILE))


def pair_product(ids, own, other, state):
    square = pltpu.VMEM((COARSE, COARSE), jnp.float32)
    return pl.pallas_call(
        pair_kernel,
        cost_estimate=cost(3),
        out_shape=(
            jax.ShapeDtypeStruct((COARSE, COARSE), jnp.float32),
            jax.ShapeDtypeStruct((HALF, COARSE), jnp.float32),
            jax.ShapeDtypeStruct((LOCAL + 8, COARSE), jnp.float32),
        ),
        in_specs=[SMEM, HBM, HBM, HBM],
        out_specs=(VMEM, VMEM, VMEM),
        scratch_shapes=[
            square,
            square,
            pltpu.VMEM((ROWS, COLS), jnp.float32),
            pltpu.VMEM((32, TILE), jnp.float32),
            pltpu.SemaphoreType.DMA((3,)),
        ],
        compiler_params=pltpu.CompilerParams(vmem_limit_bytes=24 << 20),
    )(ids, *in_hbm(own, other, state))


def fine_kernel(halo, corrected, ids_ref, class_ref, sets_ref, *refs):
    if corrected:
        c_ref, *refs = refs
        (u_ref, up_ref, f_ref, down_ref), refs = refs[:4], refs[4:]
    else:
        (up_ref, u_ref, f_ref, down_ref), refs = refs[:4], refs[4:]
    fin_ref, means_ref = refs[:2]
    u_ext, f_ext, first, second, force, coef, sums_ref, sems = refs[2:]
    ext = ROWS + 2 * halo
    lines = ext // 8
    wide = 2 * STEPS
    strip = ids_ref[0]
    if corrected:
        parts = ((u_ref, 0, ext, u_ext, 0),)
    else:
        parts = (
            (u_ref, 0, ROWS, u_ext, halo),
            (up_ref, wide - halo, halo, u_ext, 0),
            (down_ref, 0, halo, u_ext, halo + ROWS),
        )
    parts += (
        (f_ref, 0, ROWS, f_ext, halo),
        (up_ref, 2 * wide - halo, halo, f_ext, 0),
        (down_ref, wide, halo, f_ext, halo + ROWS),
    )
    copies = []
    for k in range(TILES):
        cols = pl.ds(k * TILE, TILE)
        copies.append([])
        for n, (source, at, rows, target, to) in enumerate(parts):
            copy = pltpu.make_async_copy(source.at[pl.ds(at, rows), cols], target.at[k, pl.ds(to, rows)], sems.at[n, k])
            copy.start()
            copies[k].append(copy)

    sub = iota((8, TILE), 0)
    lane = iota((8, TILE), 1)
    strips = (lax.rem(strip + 7, 8), strip, lax.rem(strip + 1, 8))

    def weights(row, k):
        label = class_ref[row, k]
        spread, along_cols, along_rows = sets_ref[0, label], sets_ref[1, label], sets_ref[2, label]
        left = STEP * (spread + jnp.maximum(along_cols, 0.0))
        right = STEP * (spread - jnp.minimum(along_cols, 0.0))
        above = STEP * (spread + jnp.maximum(along_rows, 0.0))
        below = STEP * (spread - jnp.minimum(along_rows, 0.0))
        return 1.0 - (left + right + above + below), left, right, above, below

    kinds = []
    for i in range(lines):
        kind = (i < halo, i >= lines - halo)
        if kind not in kinds:
            kinds.append(kind)
    for k in range(TILES):
        upper, inner, lower = (weights(row, k) for row in strips)
        for n, (top, bottom) in enumerate(kinds):
            for w in range(5):
                value = jnp.full((8, TILE), inner[w], jnp.float32)
                if top:
                    value = jnp.where(sub == 0, upper[w], value)
                if bottom:
                    value = jnp.where(sub == 7, lower[w], value)
                coef[k, 5 * n + w] = value

    for k in range(TILES):
        for copy in copies[k]:
            copy.wait()
        if corrected:
            added = []
            for line in range(4):
                at = lax.rem(2 * strip + 15 + line, 16) * 32 + 2 * k
                added.append(jnp.where(lane < BLK, c_ref[0, at], c_ref[0, at + 1]))
        for i in range(lines):
            value = u_ext[k, pl.ds(i, 8, stride=lines), :]
            if corrected:
                row = sub * lines + i
                addend = jnp.where(row < halo + BLK, added[1], added[2])
                if i < halo:
                    addend = jnp.where(sub == 0, added[0], addend)
                if i >= lines - halo:
                    addend = jnp.where(sub == 7, added[3], addend)
                value = value + addend
            first[k, pl.ds(i * 8, 8), :] = value
            force[k, pl.ds(i * 8, 8), :] = STEP * f_ext[k, pl.ds(i, 8, stride=lines), :]

    def tile_step(old, new, k):
        before = lax.rem(k + TILES - 1, TILES)
        after = lax.rem(k + 1, TILES)
        line = [old[k, pl.ds(i * 8, 8), :] for i in range(lines)]
        top = pltpu.roll(line[-1], 1, 0)
        bottom = pltpu.roll(line[0], 7, 0)
        for i in range(lines):
            kind = kinds.index((i < halo, i >= lines - halo))
            centre, w_left, w_right, w_above, w_below = (coef[k, 5 * kind + w] for w in range(5))
            rows = pl.ds(i * 8, 8)
            left = pltpu.roll(jnp.where(lane == TILE - 1, old[before, rows, :], line[i]), 1, 1)
            right = pltpu.roll(jnp.where(lane == 0, old[after, rows, :], line[i]), TILE - 1, 1)
            above = line[i - 1] if i else top
            below = line[i + 1] if i + 1 < lines else bottom
            new[k, rows, :] = (
                (centre * line[i] + force[k, rows, :])
                + (w_left * left + w_right * right)
                + (w_above * above + w_below * below)
            )

    def two_steps(_, carry):
        def there(k, carry):
            tile_step(first, second, k)
            return carry

        def back(k, carry):
            tile_step(second, first, k)
            return carry

        lax.fori_loop(0, TILES, there, 0, unroll=8)
        lax.fori_loop(0, TILES, back, 0, unroll=8)
        return carry

    lax.fori_loop(0, STEPS // 2, two_steps, 0)

    kept = ext - 2 * STEPS
    results = []
    for k in range(TILES):
        for i in range(lines):
            u_ext[k, pl.ds(i, 8, stride=lines), :] = first[k, pl.ds(i * 8, 8), :]
        cols = pl.ds(k * TILE, TILE)
        result = pltpu.make_async_copy(u_ext.at[k, pl.ds(STEPS, kept)], fin_ref.at[:, cols], sems.at[0, k])
        result.start()
        results.append(result)
        for br in range(2):
            part = u_ext[k, halo + br * BLK : halo + (br + 1) * BLK, :]
            sums_ref[br * TILES + k : br * TILES + k + 1, :] = jnp.sum(part, axis=0, keepdims=True)
    means_ref[...] = packed_means(sums_ref[...])
    for result in results:
        result.wait()


def fine_sweep(ids, tile_class, coeff_sets, fields, correction=None):
    corrected = correction is not None
    halo = STEPS if corrected else 2 * STEPS
    ext = ROWS + 2 * halo
    field = pltpu.VMEM((TILES, ext, TILE), jnp.float32)
    return pl.pallas_call(
        functools.partial(fine_kernel, halo, corrected),
        cost_estimate=cost(10),
        out_shape=(
            jax.ShapeDtypeStruct((ext - 2 * STEPS, COLS), jnp.float32),
            jax.ShapeDtypeStruct((1, TILE), jnp.float32),
        ),
        in_specs=[SMEM, SMEM, SMEM] + [SMEM] * corrected + [HBM] * 4,
        out_specs=(HBM, VMEM),
        scratch_shapes=[
            field,
            field,
            field,
            field,
            field,
            pltpu.VMEM((TILES, 15, 8, TILE), jnp.float32),
            pltpu.VMEM((32, TILE), jnp.float32),
            pltpu.SemaphoreType.DMA((6, TILES)),
        ],
        compiler_params=pltpu.CompilerParams(vmem_limit_bytes=32 << 20),
    )(ids, tile_class, coeff_sets, *([correction] * corrected), *in_hbm(*fields))


def message_kernel(ids_ref, means_ref, base_ref, columns_ref, out_ref, block):
    defect = means_ref[...] - base_ref[...]
    lane = iota((1, TILE), 1)
    pushed = jnp.dot(
        jnp.broadcast_to(defect, (8, TILE))[:, :LOCAL],
        columns_ref[0:LOCAL, :],
        precision=HIGHEST,
        preferred_element_type=jnp.float32,
    )
    odd = lax.rem(ids_ref[0], 2)
    raw = jnp.where((lane >= LOCAL) == (odd == 1), defect, 0.0)
    pieces = [pushed[0:1, q * TILE : (q + 1) * TILE] for q in range(4)] + [raw]
    for n in range(8):
        for q in range(PIECES):
            block[n * PIECES + q : n * PIECES + q + 1, :] = pieces[q]
    for n in range(16):
        out_ref[n * 8 * PIECES : (n + 1) * 8 * PIECES, :] = block[...]


def message(ids, means, base, columns):
    return pl.pallas_call(
        message_kernel,
        cost_estimate=cost(1),
        out_shape=jax.ShapeDtypeStruct((128 * PIECES, TILE), jnp.float32),
        in_specs=[SMEM, VMEM, VMEM, VMEM],
        out_specs=VMEM,
        scratch_shapes=[pltpu.VMEM((8 * PIECES, TILE), jnp.float32)],
        compiler_params=pltpu.CompilerParams(vmem_limit_bytes=16 << 20),
    )(ids, means, base, columns)


def chain_kernel(last, ids_ref, got_ref, other_ref, *refs):
    whole, refs = refs[:5], refs[5:]
    halved, refs = refs[:6], refs[6:]
    if last:
        u_ref, refs = refs[0], refs[1:]
    out_ref, refs = refs[0], refs[1:]
    if not last:
        local_ref, refs = refs[0], refs[1:]
    maps, early, sems, *refs = refs
    strip, core, chip, y = ids_ref[0], ids_ref[1], ids_ref[2], ids_ref[3]

    def fetch_whole(slot, source):
        for part in range(2):
            rows = pl.ds(part * HALF, HALF)
            pltpu.make_async_copy(source.at[rows], maps.at[slot, rows], sems.at[slot, part]).start()

    def fetch_halves(slot, which):
        for part, at in ((0, core), (1, 1 - core)):
            rows = pl.ds(pl.multiple_of(at * HALF, HALF), HALF)
            pltpu.make_async_copy(halved[2 * which + part], maps.at[slot, rows], sems.at[slot, part]).start()

    def fetch_turned(slot, pair, below):
        mine, theirs = pair
        own = (core == 0) == below

        @pl.when(own)
        def _():
            fetch_whole(slot, mine)

        @pl.when(jnp.logical_not(own))
        def _():
            fetch_whole(slot, theirs)

    def fetch_near(slot, ahead):
        if ahead == 2:
            fetch_halves(slot, 0)
        else:
            fetch_turned(slot, whole[0:2], ahead == 3)

    def fetch_far(slot, ahead):
        if ahead in (0, 2):
            fetch_halves(slot, 2 if ahead else 1)
        else:
            fetch_turned(slot, whole[2:4], ahead == 3)

    def landed(slot):
        for part in range(2):
            rows = pl.ds(0, HALF)
            pltpu.make_async_copy(other_ref.at[rows], maps.at[slot, rows], sems.at[slot, part]).wait()

    for half in range(2):
        if half == 1:
            fetch_far(4, 0)
        for ahead in range(1, 4):
            wraps = y + ahead >= 4

            @pl.when(wraps == (half == 0))
            def _():
                fetch_far(4 * half + ahead, ahead)

            @pl.when(wraps != (half == 0))
            def _():
                fetch_near(4 * half + ahead, ahead)

    fetch_whole(0, whole[4])
    final = pltpu.make_async_copy(other_ref, early, sems.at[8, 0])
    final.start()
    if last:
        u, sem = refs
        state = pltpu.make_async_copy(u_ref, u, sem)
        state.start()

    diagonal = iota((TILE, TILE), 0) == iota((TILE, TILE), 1)

    def applied(matrix, vector):
        row = jnp.concatenate(vector, axis=1)
        column = jnp.sum(matrix * row, axis=1, keepdims=True)
        return [
            jnp.sum(jnp.where(diagonal, column[q * TILE : (q + 1) * TILE], 0.0), axis=0, keepdims=True)
            for q in range(4)
        ]

    def group(window):
        start = lax.rem(window + 16, 16) * (8 * PIECES)
        return [
            jnp.sum(got_ref[pl.ds(start + q, 8, stride=PIECES), :], axis=0, keepdims=True) for q in range(4)
        ]

    def add(a, b):
        return [p + q for p, q in zip(a, b, strict=True)]

    def pushed(step):
        at = 2 * lax.rem(chip + step, 8)
        return add(group(at - 1), group(at))

    value = [jnp.where(core == 1, p, q) for p, q in zip(group(2 * chip), pushed(0), strict=True)]

    def arriving(step, value):
        landed(step)
        return add(applied(maps[step], value), pushed(step))

    value = lax.fori_loop(1, 8, arriving, value)
    landed(0)

    def again(step, value):
        return add(applied(maps[step], value), pushed(step))

    value = lax.fori_loop(0, 8, again, value)
    final.wait()
    start = lax.rem(2 * chip + 15, 16) * (8 * PIECES) + 4
    raw = got_ref[pl.ds(start, 8, stride=PIECES), :]
    defect = [raw[2 * q : 2 * q + 1] + raw[2 * q + 1 : 2 * q + 2] for q in range(4)]
    value = [
        jnp.where(core == 1, p, q) for p, q in zip(applied(early[...], add(value, defect)), value, strict=True)
    ]
    if not last:
        out_ref[...] = jnp.concatenate(value, axis=1)
    lane = iota((8, TILE), 1)
    piece = value[3]
    for q in range(3):
        piece = jnp.where(strip // 2 == q, value[q], piece)
    piece = jnp.broadcast_to(piece, (8, TILE))
    odd = lax.rem(strip, 2)
    if not last:
        here = jnp.where((lane < LOCAL) == (odd == 0), piece, pltpu.roll(piece, LOCAL, 1))
        local_ref[...] = jnp.broadcast_to(here[0:1], (2 * TILE, TILE))
        return
    state.wait()
    outs = []
    for k in range(TILES):
        cols = slice(k * TILE, (k + 1) * TILE)
        for br in range(2):
            at = odd * LOCAL + br * 32 + 2 * k
            added = jnp.take_along_axis(piece, at + jnp.where(lane < BLK, 0, 1), axis=1)
            for n in range(BLK // 8):
                rows = slice(br * BLK + n * 8, br * BLK + (n + 1) * 8)
                u[rows, cols] = u[rows, cols] + added
        if k % 4 == 3:
            cols = pl.ds((k - 3) * TILE, 4 * TILE)
            copy = pltpu.make_async_copy(u.at[:, cols], out_ref.at[:, cols], sems.at[k // 4, 0])
            copy.start()
            outs.append(copy)
    for copy in outs:
        copy.wait()


def chain(ids, got, other, whole, halved, previous=None):
    last = previous is not None
    if last:
        out_shape, out_specs = jax.ShapeDtypeStruct((ROWS, COLS), jnp.float32), HBM
    else:
        out_shape = (
            jax.ShapeDtypeStruct((1, COARSE), jnp.float32),
            jax.ShapeDtypeStruct((2 * TILE, TILE), jnp.float32),
        )
        out_specs = (VMEM, VMEM)
    return pl.pallas_call(
        functools.partial(chain_kernel, last),
        cost_estimate=cost(5),
        out_shape=out_shape,
        in_specs=[SMEM, VMEM] + [HBM] * (12 + last),
        out_specs=out_specs,
        scratch_shapes=[
            pltpu.VMEM((8, COARSE, COARSE), jnp.float32),
            pltpu.VMEM((COARSE, COARSE), jnp.float32),
            pltpu.SemaphoreType.DMA((9, 2)),
        ]
        + [pltpu.VMEM((ROWS, COLS), jnp.float32), pltpu.SemaphoreType.DMA] * last,
        compiler_params=pltpu.CompilerParams(vmem_limit_bytes=32 << 20),
    )(ids, got, *in_hbm(other, *whole, *halved, *([previous] * last)))


def exchanged(block):
    block = block.reshape(128, 1, PIECES * TILE)
    return lax.all_to_all(block, ("tm", "space"), 0, 0, tiled=True).reshape(128 * PIECES, TILE)


def swapped(value):
    return moved(value, lambda x, y, z, core: (x, y, z, 1 - core))


def across(value):
    return moved(value, lambda x, y, z, core: (x, y, z + 1 - 2 * core, core))


def along(value, dz=0):
    return moved(value, lambda x, y, z, core: (x, y + 1 - 2 * core, z + dz * (1 - 2 * core), core))


def per_device(initial_states, sources, tile_class, coeff_sets, coarse_maps):
    state, source, own_map = initial_states[0], sources[0], coarse_maps[0]
    window = lax.axis_index("tm").astype(jnp.int32)
    strip = lax.axis_index("space").astype(jnp.int32)
    core = window % 2
    ids = jnp.stack([strip, core, window // 2, (window // 2) % 4])
    wide = 2 * STEPS

    other_map = swapped(own_map)
    upper = shifted(jnp.concatenate([state[-wide:], source[-wide:]], axis=0), 0, 1)
    lower = shifted(jnp.concatenate([state[:wide], source[:wide]], axis=0), 0, -1)

    product, half, columns = pair_product(ids, own_map, other_map, state)
    product, half, columns, upper, lower = lax.optimization_barrier((product, half, columns, upper, lower))
    near = along(product)
    far_same = across(half)
    columns = shifted(columns, -1)

    finished, means = fine_sweep(ids, tile_class, coeff_sets, (upper, state, source, lower))
    near, far_same, columns, means, finished = lax.optimization_barrier(
        (near, far_same, columns, means, finished)
    )
    near_half = lax.dynamic_slice(near, (core * HALF, 0), (HALF, COARSE))
    far = across(near)
    near_second = along(near_half)
    far_second = along(near_half, 1)

    got = exchanged(message(ids, means, columns[LOCAL : LOCAL + 1, :TILE], columns))

    got, far, near_second, far_second, finished = lax.optimization_barrier(
        (got, far, near_second, far_second, finished)
    )
    previous = shifted(finished, 1)
    whole = [near, swapped(near), far, swapped(far), product]
    halved = []
    for part in (near_second, far_same, far_second):
        halved += [part, swapped(part)]
    correction, local = chain(ids, got, other_map, whole, halved)

    base = means + shifted(local, -1)[:1]
    finished, means = fine_sweep(ids, tile_class, coeff_sets, (previous, upper, source, lower), correction)
    previous = shifted(finished, 1)
    got = exchanged(message(ids, means, base, columns))
    return chain(ids, got, other_map, whole, halved, previous)[None]


def solution(mesh):
    placed = (P("tm", "space", None), P("tm", "space", None), P(), P(), P("tm", None, None))
    return jax.shard_map(
        per_device, mesh=mesh, in_specs=placed, out_specs=P("tm", "space", None), check_vma=False
    )
```

```python
import functools

import jax
import jax.numpy as jnp
from jax import lax
from jax.experimental import pallas as pl
from jax.experimental.pallas import tpu as pltpu
from jax.sharding import PartitionSpec as P

TILE = 128
BLK = 64
STEPS = 8
ROWS = 128
COLS = 2048
COARSE = 512
HALF = COARSE // 2
TILES = COLS // TILE
LOCAL = 64
PIECES = 5
STEP = 0.6

HIGHEST = lax.Precision.HIGHEST
HBM = pl.BlockSpec(memory_space=pltpu.HBM)
ANY = pl.BlockSpec(memory_space=pl.ANY)
SMEM = pl.BlockSpec(memory_space=pltpu.SMEM)
VMEM = pl.BlockSpec(memory_space=pltpu.VMEM)


def place(device):
    tm, space = divmod(device, 8)
    z_lo, rest = divmod(tm, 8)
    y, core = divmod(rest, 2)
    z_hi, x = divmod(space, 4)
    return x, y, 2 * z_hi + z_lo, core


def device_at(x, y, z, core):
    x, y, z, core = x % 4, y % 4, z % 4, core % 2
    return ((z % 2) * 8 + y * 2 + core) * 8 + (z // 2) * 4 + x


def moved(value, route):
    pairs = [(i, device_at(*route(*place(i)))) for i in range(128)]
    return lax.ppermute(value, ("tm", "space"), pairs)


def shifted(value, windows, strips=0):
    pairs = [
        (tm * 8 + sp, (tm + windows) % 16 * 8 + (sp + strips) % 8)
        for tm in range(16)
        for sp in range(8)
    ]
    return lax.ppermute(value, ("tm", "space"), pairs)


def cost(micros):
    return pl.CostEstimate(flops=0, transcendentals=0, bytes_accessed=int(micros * 3.6e6))


def in_hbm(*values):
    return [pltpu.with_memory_space_constraint(value, pltpu.HBM) for value in values]


def position():
    window = lax.axis_index("tm")
    pair = window // 2
    return lax.axis_index("space"), lax.rem(window, 2), pair, lax.rem(pair, 4)


def iota(shape, axis):
    return lax.broadcasted_iota(jnp.int32, shape, axis)


def packed_means(sums):
    lane = iota((32, TILE), 1)
    row = iota((32, TILE), 0)
    low = jnp.sum(jnp.where(lane < BLK, sums, 0.0), axis=1, keepdims=True)
    high = jnp.sum(jnp.where(lane < BLK, 0.0, sums), axis=1, keepdims=True)
    slot = lane & (LOCAL - 1)
    spread = jnp.where(slot == 2 * row, low, 0.0) + jnp.where(slot == 2 * row + 1, high, 0.0)
    return jnp.sum(spread, axis=0, keepdims=True) * (1.0 / (BLK * BLK))


def fill_weights(strip, class_ref, sets_ref, coef_ref):
    sub = iota((8, TILE), 0)
    strips = (lax.rem(strip + 7, 8), strip, lax.rem(strip + 1, 8))

    def weights(row, k):
        label = class_ref[row, k]
        spread, along_cols, along_rows = sets_ref[0, label], sets_ref[1, label], sets_ref[2, label]
        left = STEP * (spread + jnp.maximum(along_cols, 0.0))
        right = STEP * (spread - jnp.minimum(along_cols, 0.0))
        above = STEP * (spread + jnp.maximum(along_rows, 0.0))
        below = STEP * (spread - jnp.minimum(along_rows, 0.0))
        return 1.0 - (left + right + above + below), left, right, above, below

    for k in range(TILES):
        upper, inner, lower = (weights(row, k) for row in strips)
        for w in range(5):
            value = jnp.full((8, TILE), inner[w], jnp.float32)
            with_upper = jnp.where(sub == 0, upper[w], value)
            coef_ref[k, w] = value
            coef_ref[k, 5 + w] = with_upper
            coef_ref[k, 10 + w] = jnp.where(sub == 7, lower[w], value)
            coef_ref[k, 15 + w] = jnp.where(sub == 7, lower[w], with_upper)


def pair_kernel(class_ref, sets_ref, own_ref, other_ref, u_ref, q_ref, half_ref, columns_ref, coef_ref, *scratch):
    late, early, u, sums_ref, columns, sems = scratch
    strip, core, _, _ = position()
    state = pltpu.make_async_copy(u_ref, u, sems.at[2])

    def both(first, second):
        a = pltpu.make_async_copy(first, late, sems.at[0])
        b = pltpu.make_async_copy(second, early, sems.at[1])
        a.start()
        b.start()
        state.start()
        a.wait()
        b.wait()

    @pl.when(core == 1)
    def _():
        both(own_ref, other_ref)

    @pl.when(core == 0)
    def _():
        both(other_ref, own_ref)

    fill_weights(strip, class_ref, sets_ref, coef_ref)

    def split(value):
        big = value.astype(jnp.bfloat16)
        return big, (value - big.astype(jnp.float32)).astype(jnp.bfloat16)

    def times(a, b):
        return jnp.dot(a, b, preferred_element_type=jnp.float32)

    early_big, early_small = split(early[...])
    for part in range(2):
        rows = slice(part * HALF, (part + 1) * HALF)
        big, small = split(late[rows, :])
        q_ref[rows, :] = times(big, early_big) + (times(big, early_small) + times(small, early_big))
    half_ref[...] = q_ref[pl.ds(pl.multiple_of(core * HALF, HALF), HALF), :]
    cols = pl.ds(pl.multiple_of(strip // 2 * TILE, TILE), TILE)
    wide = jnp.where(core == 1, late[:, cols], q_ref[:, cols])
    turned = jnp.transpose(wide)
    columns[0:LOCAL, :] = jnp.where(lax.rem(strip, 2) == 1, turned[LOCAL:], turned[:LOCAL])
    state.wait()
    for k in range(TILES):
        cols = slice(k * TILE, (k + 1) * TILE)
        for br in range(2):
            part = u[br * BLK : (br + 1) * BLK, cols]
            sums_ref[br * TILES + k : br * TILES + k + 1, :] = jnp.sum(part, axis=0, keepdims=True)
    columns[LOCAL:, :] = jnp.zeros((8, COARSE), jnp.float32)
    columns[LOCAL:, 0:TILE] = jnp.broadcast_to(packed_means(sums_ref[...]), (8, TILE))
    done = pltpu.make_async_copy(columns, columns_ref, sems.at[0])
    done.start()
    done.wait()


def pair_product(tile_class, coeff_sets, own, other, state):
    square = pltpu.VMEM((COARSE, COARSE), jnp.float32)
    return pl.pallas_call(
        pair_kernel,
        cost_estimate=cost(3),
        out_shape=(
            jax.ShapeDtypeStruct((COARSE, COARSE), jnp.float32),
            jax.ShapeDtypeStruct((HALF, COARSE), jnp.float32),
            pltpu.HBM((LOCAL + 8, COARSE), jnp.float32),
            jax.ShapeDtypeStruct((TILES, 20, 8, TILE), jnp.float32),
        ),
        in_specs=[SMEM, SMEM, HBM, ANY, HBM],
        out_specs=(VMEM, VMEM, HBM, VMEM),
        scratch_shapes=[
            square,
            square,
            pltpu.VMEM((ROWS, COLS), jnp.float32),
            pltpu.VMEM((32, TILE), jnp.float32),
            pltpu.VMEM((LOCAL + 8, COARSE), jnp.float32),
            pltpu.SemaphoreType.DMA((3,)),
        ],
        compiler_params=pltpu.CompilerParams(vmem_limit_bytes=24 << 20),
    )(tile_class, coeff_sets, *in_hbm(own), other, *in_hbm(state))


def fine_kernel(halo, corrected, coef, *refs):
    if corrected:
        c_ref, means_ref, own_ref, other_ref, own_columns_ref, columns_ref, u_ref, f_ref, fin_ref, out_ref, *refs = refs
        block, means_scratch, columns_scratch, extra, *refs = refs
    else:
        up_ref, u_ref, f_ref, down_ref, fin_ref, out_ref, means_ref, force_ref, *refs = refs
        means_scratch, extra, *refs = refs
    u_ext, f_ext, first, second, force, sums_ref, sems = refs
    ext = ROWS + 2 * halo
    lines = ext // 8
    wide = 2 * STEPS
    strip, core, _, _ = position()
    if corrected:
        parts = ((u_ref, 0, ext, u_ext, 0), (f_ref, 0, ext, f_ext, 0))
    else:
        parts = (
            (u_ref, 0, ROWS, u_ext, halo),
            (up_ref, wide - halo, halo, u_ext, 0),
            (down_ref, 0, halo, u_ext, halo + ROWS),
            (f_ref, 0, ROWS, f_ext, halo),
            (up_ref, 2 * wide - halo, halo, f_ext, 0),
            (down_ref, wide, halo, f_ext, halo + ROWS),
        )
    copies = []
    for k in range(TILES):
        cols = pl.ds(k * TILE, TILE)
        copies.append([])
        for n, (source, at, rows, target, to) in enumerate(parts):
            copy = pltpu.make_async_copy(source.at[pl.ds(at, rows), cols], target.at[k, pl.ds(to, rows)], sems.at[n, k])
            copy.start()
            copies[k].append(copy)

    if corrected:
        needed = [
            pltpu.make_async_copy(means_ref, means_scratch, extra.at[0]),
            pltpu.make_async_copy(own_columns_ref, columns_scratch, extra.at[1]),
        ]
        for copy in needed:
            copy.start()
    sub = iota((8, TILE), 0)
    lane = iota((8, TILE), 1)

    results = []
    for k in range(TILES):
        for copy in copies[k]:
            copy.wait()
        if not corrected:
            cols = pl.ds(k * TILE, TILE)
            result = pltpu.make_async_copy(f_ext.at[k, pl.ds(STEPS, ext - 2 * STEPS)], force_ref.at[:, cols], extra.at[1, k])
            result.start()
            results.append(result)
        if corrected:
            added = []
            for line in range(4):
                at = lax.rem(2 * strip + 15 + line, 16) * 32 + 2 * k
                added.append(jnp.where(lane < BLK, c_ref[0, at], c_ref[0, at + 1]))
        for i in range(lines):
            value = u_ext[k, pl.ds(i, 8, stride=lines), :]
            if corrected:
                row = sub * lines + i
                addend = jnp.where(row < halo + BLK, added[1], added[2])
                if i < halo:
                    addend = jnp.where(sub == 0, added[0], addend)
                if i >= lines - halo:
                    addend = jnp.where(sub == 7, added[3], addend)
                value = value + addend
            first[k, pl.ds(i * 8, 8), :] = value
            force[k, pl.ds(i * 8, 8), :] = STEP * f_ext[k, pl.ds(i, 8, stride=lines), :]

    def tile_step(old, new, k):
        before = lax.rem(k + TILES - 1, TILES)
        after = lax.rem(k + 1, TILES)
        line = [old[k, pl.ds(i * 8, 8), :] for i in range(lines)]
        top = pltpu.roll(line[-1], 1, 0)
        bottom = pltpu.roll(line[0], 7, 0)
        for i in range(lines):
            kind = (i < halo) + 2 * (i >= lines - halo)
            centre, w_left, w_right, w_above, w_below = (coef[k, 5 * kind + w] for w in range(5))
            rows = pl.ds(i * 8, 8)
            left = pltpu.roll(jnp.where(lane == TILE - 1, old[before, rows, :], line[i]), 1, 1)
            right = pltpu.roll(jnp.where(lane == 0, old[after, rows, :], line[i]), TILE - 1, 1)
            above = line[i - 1] if i else top
            below = line[i + 1] if i + 1 < lines else bottom
            new[k, rows, :] = (
                (centre * line[i] + force[k, rows, :])
                + (w_left * left + w_right * right)
                + (w_above * above + w_below * below)
            )

    def two_steps(_, carry):
        def there(k, carry):
            tile_step(first, second, k)
            return carry

        def back(k, carry):
            tile_step(second, first, k)
            return carry

        lax.fori_loop(0, TILES, there, 0, unroll=8)
        lax.fori_loop(0, TILES, back, 0, unroll=8)
        return carry

    lax.fori_loop(0, STEPS // 2, two_steps, 0)

    kept = ext - 2 * STEPS
    for k in range(TILES):
        for i in range(lines):
            u_ext[k, pl.ds(i, 8, stride=lines), :] = first[k, pl.ds(i * 8, 8), :]
        cols = pl.ds(k * TILE, TILE)
        result = pltpu.make_async_copy(u_ext.at[k, pl.ds(STEPS, kept)], fin_ref.at[:, cols], sems.at[0, k])
        result.start()
        results.append(result)
        for br in range(2):
            part = u_ext[k, halo + br * BLK : halo + (br + 1) * BLK, :]
            sums_ref[br * TILES + k : br * TILES + k + 1, :] = jnp.sum(part, axis=0, keepdims=True)
    means = packed_means(sums_ref[...])
    if corrected:
        for copy in needed:
            copy.wait()
        grown = means - means_scratch[...]
        even = core == 0
        pushed = rows_times(grown - jnp.where(even, other_ref[...], 0.0), columns_ref[0:LOCAL, :])
        pushed = pushed - rows_times(jnp.where(even, own_ref[...], 0.0), columns_scratch[0:LOCAL, :])
        write_message(strip, pushed, grown, block, out_ref)
    else:
        out_ref[...] = means
        means_scratch[...] = means
        result = pltpu.make_async_copy(means_scratch, means_ref, extra.at[0, 0])
        result.start()
        results.append(result)
    for result in results:
        result.wait()


def fine_call(halo, corrected, in_specs, more_out, more_specs, scratch, args):
    ext = ROWS + 2 * halo
    field = pltpu.VMEM((TILES, ext, TILE), jnp.float32)
    return pl.pallas_call(
        functools.partial(fine_kernel, halo, corrected),
        cost_estimate=cost(10),
        out_shape=(pltpu.HBM((ext - 2 * STEPS, COLS), jnp.float32), *more_out),
        in_specs=in_specs,
        out_specs=(HBM, *more_specs),
        scratch_shapes=[
            *scratch,
            field,
            field,
            field,
            field,
            field,
            pltpu.VMEM((32, TILE), jnp.float32),
            pltpu.SemaphoreType.DMA((6, TILES)),
        ],
        compiler_params=pltpu.CompilerParams(vmem_limit_bytes=16 << 20),
    )(*args)


def first_sweep(coef, upper, state, source, lower):
    state, source = in_hbm(state, source)
    return fine_call(
        2 * STEPS,
        False,
        [VMEM] + [ANY] * 4,
        (
            jax.ShapeDtypeStruct((1, TILE), jnp.float32),
            pltpu.HBM((1, TILE), jnp.float32),
            pltpu.HBM((ROWS + 2 * STEPS, COLS), jnp.float32),
        ),
        (VMEM, HBM, HBM),
        [pltpu.VMEM((1, TILE), jnp.float32), pltpu.SemaphoreType.DMA((2, TILES))],
        (coef, upper, state, source, lower),
    )


def second_sweep(coef, correction, means, own_part, other_part, columns, next_columns, state, sources):
    means, columns, sources = in_hbm(means, columns, sources)
    return fine_call(
        STEPS,
        True,
        [VMEM, SMEM, HBM, VMEM, VMEM, HBM, VMEM, ANY, HBM],
        (jax.ShapeDtypeStruct((128 * PIECES, TILE), jnp.float32),),
        (VMEM,),
        [
            pltpu.VMEM((8 * PIECES, TILE), jnp.float32),
            pltpu.VMEM((1, TILE), jnp.float32),
            pltpu.VMEM((LOCAL + 8, COARSE), jnp.float32),
            pltpu.SemaphoreType.DMA((2,)),
        ],
        (coef, correction, means, own_part, other_part, columns, next_columns, state, sources),
    )


def rows_times(row, matrix):
    row = jnp.broadcast_to(row, (8, TILE))[:, :LOCAL]
    return jnp.dot(row, matrix, precision=HIGHEST, preferred_element_type=jnp.float32)


def write_message(strip, pushed, raw, block, out_ref):
    lane = iota((1, TILE), 1)
    raw = jnp.where((lane >= LOCAL) == (lax.rem(strip, 2) == 1), raw, 0.0)
    pieces = [pushed[0:1, q * TILE : (q + 1) * TILE] for q in range(4)] + [raw]
    for n in range(8):
        for q in range(PIECES):
            block[n * PIECES + q : n * PIECES + q + 1, :] = pieces[q]
    for n in range(16):
        out_ref[n * 8 * PIECES : (n + 1) * 8 * PIECES, :] = block[...]


def message_kernel(means_ref, base_ref, columns_ref, out_ref, block):
    defect = means_ref[...] - base_ref[...]
    strip, _, _, _ = position()
    write_message(strip, rows_times(defect, columns_ref[0:LOCAL, :]), defect, block, out_ref)


def message(means, base, columns):
    return pl.pallas_call(
        message_kernel,
        cost_estimate=cost(1),
        out_shape=jax.ShapeDtypeStruct((128 * PIECES, TILE), jnp.float32),
        in_specs=[VMEM, VMEM, VMEM],
        out_specs=VMEM,
        scratch_shapes=[pltpu.VMEM((8 * PIECES, TILE), jnp.float32)],
        compiler_params=pltpu.CompilerParams(vmem_limit_bytes=16 << 20),
    )(means, base, columns)


def add(a, b):
    return [p + q for p, q in zip(a, b, strict=True)]


def minus(a, b):
    return [p - q for p, q in zip(a, b, strict=True)]


def select(condition, a, b):
    return [jnp.where(condition, p, q) for p, q in zip(a, b, strict=True)]


def quarters(row):
    return [row[:, q * TILE : (q + 1) * TILE] for q in range(4)]


def applied(matrix, vector):
    diagonal = iota((TILE, TILE), 0) == iota((TILE, TILE), 1)
    column = jnp.sum(matrix * jnp.concatenate(vector, axis=1), axis=1, keepdims=True)
    return [
        jnp.sum(jnp.where(diagonal, column[q * TILE : (q + 1) * TILE], 0.0), axis=0, keepdims=True) for q in range(4)
    ]


def pushes(got_ref, window):
    start = lax.rem(window + 16, 16) * (8 * PIECES)
    return [jnp.sum(got_ref[pl.ds(start + q, 8, stride=PIECES), :], axis=0, keepdims=True) for q in range(4)]


def gathered(got_ref, window):
    start = lax.rem(window + 16, 16) * (8 * PIECES) + 4
    raw = got_ref[pl.ds(start, 8, stride=PIECES), :]
    return [raw[2 * q : 2 * q + 1] + raw[2 * q + 1 : 2 * q + 2] for q in range(4)]


def pair_pushes(got_ref, pair):
    at = 2 * lax.rem(pair, 8)
    return add(pushes(got_ref, at - 1), pushes(got_ref, at))


def strip_piece(strip, value):
    piece = value[3]
    for q in range(3):
        piece = jnp.where(strip // 2 == q, value[q], piece)
    return jnp.broadcast_to(piece, (8, TILE))


def first_chain_kernel(got_ref, other_ref, *refs):
    whole, halved = refs[:5], refs[5:11]
    out_ref, maps_ref, maps, sems, out_sems = refs[11:]
    strip, core, chip, y = position()

    def fetch(slot, source):
        for part in range(2):
            rows = pl.ds(part * HALF, HALF)
            pltpu.make_async_copy(source.at[rows], maps.at[slot, rows], sems.at[slot, part]).start()

    def fetch_halves(slot, which):
        for part, at in ((0, core), (1, 1 - core)):
            rows = pl.ds(pl.multiple_of(at * HALF, HALF), HALF)
            pltpu.make_async_copy(halved[2 * which + part], maps.at[slot, rows], sems.at[slot, part]).start()

    def fetch_turned(slot, pair, below):
        own = (core == 0) == below

        @pl.when(own)
        def _():
            fetch(slot, pair[0])

        @pl.when(jnp.logical_not(own))
        def _():
            fetch(slot, pair[1])

    def fetch_near(slot, ahead):
        if ahead == 2:
            fetch_halves(slot, 0)
        else:
            fetch_turned(slot, whole[0:2], ahead == 3)

    def fetch_far(slot, ahead):
        if ahead in (0, 2):
            fetch_halves(slot, 2 if ahead else 1)
        else:
            fetch_turned(slot, whole[2:4], ahead == 3)

    def landed(slot):
        for part in range(2):
            rows = pl.ds(0, HALF)
            pltpu.make_async_copy(whole[4].at[rows], maps.at[slot, rows], sems.at[slot, part]).wait()
        kept(slot).start()

    def kept(slot):
        return pltpu.make_async_copy(maps.at[slot], maps_ref.at[slot], out_sems.at[slot])

    for half in range(2):
        if half == 1:
            fetch_far(4, 0)
        for ahead in range(1, 4):
            wraps = y + ahead >= 4

            @pl.when(wraps == (half == 0))
            def _():
                fetch_far(4 * half + ahead, ahead)

            @pl.when(wraps != (half == 0))
            def _():
                fetch_near(4 * half + ahead, ahead)

    fetch(0, whole[4])
    fetch(8, other_ref)
    value = select(core == 1, pushes(got_ref, 2 * chip), pair_pushes(got_ref, chip))

    def arriving(step, value):
        landed(step)
        return add(applied(maps[step], value), pair_pushes(got_ref, chip + step))

    value = lax.fori_loop(1, 8, arriving, value)
    landed(0)
    landed(8)

    def again(step, value):
        return add(applied(maps[step], value), pair_pushes(got_ref, chip + step))

    value = lax.fori_loop(0, 8, again, value)
    value = select(core == 1, applied(maps[8], add(value, gathered(got_ref, 2 * chip + 15))), value)
    piece = strip_piece(strip, value)
    lane = iota((8, TILE), 1)
    here = jnp.where((lane < LOCAL) == (lax.rem(strip, 2) == 0), piece, pltpu.roll(piece, LOCAL, 1))
    out_ref[...] = jnp.concatenate(value + [here[0:1]], axis=1)
    for slot in range(9):
        kept(slot).wait()


def first_chain(got, other, whole, halved):
    return pl.pallas_call(
        first_chain_kernel,
        cost_estimate=cost(5),
        out_shape=(
            jax.ShapeDtypeStruct((1, COARSE + TILE), jnp.float32),
            pltpu.HBM((9, COARSE, COARSE), jnp.float32),
        ),
        in_specs=[VMEM] + [ANY] * 12,
        out_specs=(VMEM, HBM),
        scratch_shapes=[
            pltpu.VMEM((9, COARSE, COARSE), jnp.float32),
            pltpu.SemaphoreType.DMA((9, 2)),
            pltpu.SemaphoreType.DMA((9,)),
        ],
        compiler_params=pltpu.CompilerParams(vmem_limit_bytes=16 << 20),
    )(got, other, *whole, *halved)


def last_chain_kernel(got_ref, own_ref, partner_ref, late_ref, maps_ref, u_ref, out_ref, late, maps, sems, u, sem, out_sems):
    strip, core, chip, _ = position()

    def fetched(slot):
        return pltpu.make_async_copy(maps_ref.at[slot], maps.at[slot], sems.at[slot])

    first = pltpu.make_async_copy(late_ref, late, sems.at[9])
    first.start()
    for slot in (1, 2, 3, 4, 5, 6, 7, 0, 8):
        fetched(slot).start()
    state = pltpu.make_async_copy(u_ref, u, sem)
    state.start()
    own, partner = quarters(own_ref[...]), quarters(partner_ref[...])
    even_start = pair_pushes(got_ref, chip)
    odd_start = minus(gathered(got_ref, 2 * chip), own)
    first.wait()
    value = select(core == 1, applied(late[...], odd_start), even_start)

    def arriving(step, value):
        fetched(step).wait()
        return add(applied(maps[step], value), pair_pushes(got_ref, chip + step))

    value = lax.fori_loop(1, 8, arriving, value)
    fetched(0).wait()

    def again(step, value):
        return add(applied(maps[step], value), pair_pushes(got_ref, chip + step))

    value = lax.fori_loop(0, 8, again, value)
    fetched(8).wait()
    final = applied(maps[8], add(value, minus(gathered(got_ref, 2 * chip + 15), partner)))
    piece = strip_piece(strip, select(core == 1, final, value))
    state.wait()
    lane = iota((8, TILE), 1)
    outs = []
    for k in range(TILES):
        cols = slice(k * TILE, (k + 1) * TILE)
        for br in range(2):
            at = lax.rem(strip, 2) * LOCAL + br * 32 + 2 * k
            added = jnp.take_along_axis(piece, at + jnp.where(lane < BLK, 0, 1), axis=1)
            for n in range(BLK // 8):
                rows = slice(br * BLK + n * 8, br * BLK + (n + 1) * 8)
                u[rows, cols] = u[rows, cols] + added
        if k % 4 == 3:
            cols = pl.ds((k - 3) * TILE, 4 * TILE)
            copy = pltpu.make_async_copy(u.at[:, cols], out_ref.at[:, cols], out_sems.at[k // 4])
            copy.start()
            outs.append(copy)
    for copy in outs:
        copy.wait()


def last_chain(got, own, partner, late, maps, previous):
    square = (COARSE, COARSE)
    return pl.pallas_call(
        last_chain_kernel,
        cost_estimate=cost(6),
        out_shape=jax.ShapeDtypeStruct((ROWS, COLS), jnp.float32),
        in_specs=[VMEM, VMEM, VMEM, HBM, HBM, ANY],
        out_specs=HBM,
        scratch_shapes=[
            pltpu.VMEM(square, jnp.float32),
            pltpu.VMEM((9, *square), jnp.float32),
            pltpu.SemaphoreType.DMA((10,)),
            pltpu.VMEM((ROWS, COLS), jnp.float32),
            pltpu.SemaphoreType.DMA,
            pltpu.SemaphoreType.DMA((4,)),
        ],
        compiler_params=pltpu.CompilerParams(vmem_limit_bytes=16 << 20),
    )(got, own, partner, *in_hbm(late, maps), previous)


def exchanged(block):
    block = block.reshape(128, 1, PIECES * TILE)
    return lax.all_to_all(block, ("tm", "space"), 0, 0, tiled=True).reshape(128 * PIECES, TILE)


def swapped(value):
    return moved(value, lambda x, y, z, core: (x, y, z, 1 - core))


def across(value):
    return moved(value, lambda x, y, z, core: (x, y, z + 1 - 2 * core, core))


def along(value, dz=0):
    return moved(value, lambda x, y, z, core: (x, y + 1 - 2 * core, z + dz * (1 - 2 * core), core))


def per_device(initial_states, sources, tile_class, coeff_sets, coarse_maps):
    state, source, own_map = initial_states[0], sources[0], coarse_maps[0]
    core = lax.axis_index("tm") % 2
    wide = 2 * STEPS

    other_map = swapped(own_map)
    upper = shifted(jnp.concatenate([state[-wide:], source[-wide:]], axis=0), 0, 1)
    lower = shifted(jnp.concatenate([state[:wide], source[:wide]], axis=0), 0, -1)

    product, half, columns, coef = pair_product(tile_class, coeff_sets, own_map, other_map, state)
    product, half, columns, upper, lower = lax.optimization_barrier((product, half, columns, upper, lower))
    near = along(product)
    far_same = across(half)
    next_columns = shifted(columns, -1)

    finished, means, kept_means, kept_sources = first_sweep(coef, upper, state, source, lower)
    near, far_same, next_columns, means, finished = lax.optimization_barrier(
        (near, far_same, next_columns, means, finished)
    )
    near_half = lax.dynamic_slice(near, (core * HALF, 0), (HALF, COARSE))
    far = across(near)
    near_second = along(near_half)
    far_second = along(near_half, 1)

    got = exchanged(message(means, next_columns[LOCAL : LOCAL + 1, :TILE], next_columns))

    got, far, near_second, far_second, finished = lax.optimization_barrier(
        (got, far, near_second, far_second, finished)
    )
    previous = shifted(finished, 1)
    whole = [near, swapped(near), far, swapped(far), product]
    halved = []
    for part in (near_second, far_same, far_second):
        halved += [part, swapped(part)]
    correction, maps = first_chain(got, other_map, whole, halved)
    partner = swapped(correction)
    here, there = correction[:, :COARSE], partner[:, :COARSE]
    own_part, other_part = correction[:, COARSE:], partner[:, COARSE:]

    finished, block = second_sweep(
        coef, here, kept_means, own_part, other_part, columns, next_columns, previous, kept_sources
    )
    previous = shifted(finished, 1)
    got = exchanged(block)
    return last_chain(got, here, there, own_map, maps, previous)[None]


def solution(mesh):
    placed = (P("tm", "space", None), P("tm", "space", None), P(), P(), P("tm", None, None))
    return jax.shard_map(
        per_device, mesh=mesh, in_specs=placed, out_specs=P("tm", "space", None), check_vma=False
    )
```

```python
import functools

import jax
import jax.numpy as jnp
from jax import lax
from jax.experimental import pallas as pl
from jax.experimental.pallas import tpu as pltpu
from jax.sharding import PartitionSpec as P

TILE = 128
BLK = 64
STEPS = 8
ROWS = 128
COLS = 2048
COARSE = 512
HALF = COARSE // 2
TILES = COLS // TILE
EXT = ROWS + 2 * STEPS
LINES = EXT // 8
LOCAL = 64
PIECES = 5
STEP = 0.6

HIGHEST = lax.Precision.HIGHEST
HBM = pl.BlockSpec(memory_space=pltpu.HBM)
ANY = pl.BlockSpec(memory_space=pl.ANY)
SMEM = pl.BlockSpec(memory_space=pltpu.SMEM)
VMEM = pl.BlockSpec(memory_space=pltpu.VMEM)


def place(device):
    tm, space = divmod(device, 8)
    z_lo, rest = divmod(tm, 8)
    y, core = divmod(rest, 2)
    z_hi, x = divmod(space, 4)
    return x, y, 2 * z_hi + z_lo, core


def device_at(x, y, z, core):
    x, y, z, core = x % 4, y % 4, z % 4, core % 2
    return ((z % 2) * 8 + y * 2 + core) * 8 + (z // 2) * 4 + x


def moved(value, route):
    pairs = [(i, device_at(*route(*place(i)))) for i in range(128)]
    return lax.ppermute(value, ("tm", "space"), pairs)


def shifted(value, windows, strips=0):
    pairs = [
        (tm * 8 + sp, (tm + windows) % 16 * 8 + (sp + strips) % 8)
        for tm in range(16)
        for sp in range(8)
    ]
    return lax.ppermute(value, ("tm", "space"), pairs)


def cost(micros):
    return pl.CostEstimate(flops=0, transcendentals=0, bytes_accessed=int(micros * 3.6e6))


def in_hbm(*values):
    return [pltpu.with_memory_space_constraint(value, pltpu.HBM) for value in values]


def position():
    window = lax.axis_index("tm")
    pair = window // 2
    return lax.axis_index("space"), lax.rem(window, 2), pair, lax.rem(pair, 4)


def iota(shape, axis):
    return lax.broadcasted_iota(jnp.int32, shape, axis)


def packed_means(sums):
    lane = iota((32, TILE), 1)
    row = iota((32, TILE), 0)
    low = jnp.sum(jnp.where(lane < BLK, sums, 0.0), axis=1, keepdims=True)
    high = jnp.sum(jnp.where(lane < BLK, 0.0, sums), axis=1, keepdims=True)
    slot = lane & (LOCAL - 1)
    spread = jnp.where(slot == 2 * row, low, 0.0) + jnp.where(slot == 2 * row + 1, high, 0.0)
    return jnp.sum(spread, axis=0, keepdims=True) * (1.0 / (BLK * BLK))


def fill_weights(strip, class_ref, sets_ref, coef_ref):
    sub = iota((8, TILE), 0)
    strips = (lax.rem(strip + 7, 8), strip, lax.rem(strip + 1, 8))

    def weights(row, k):
        label = class_ref[row, k]
        spread, along_cols, along_rows = sets_ref[0, label], sets_ref[1, label], sets_ref[2, label]
        left = STEP * (spread + jnp.maximum(along_cols, 0.0))
        right = STEP * (spread - jnp.minimum(along_cols, 0.0))
        above = STEP * (spread + jnp.maximum(along_rows, 0.0))
        below = STEP * (spread - jnp.minimum(along_rows, 0.0))
        return 1.0 - (left + right + above + below), left, right, above, below

    for k in range(TILES):
        upper, inner, lower = (weights(row, k) for row in strips)
        for w in range(5):
            value = jnp.full((8, TILE), inner[w], jnp.float32)
            coef_ref[k, w] = value
            coef_ref[k, 5 + w] = jnp.where(sub == 0, upper[w], value)
            coef_ref[k, 10 + w] = jnp.where(sub == 7, lower[w], value)


def pair_kernel(class_ref, sets_ref, own_ref, other_ref, u_ref, q_ref, half_ref, columns_ref, coef_ref, *scratch):
    late, early, u, sums_ref, columns, sems = scratch
    strip, core, _, _ = position()
    state = pltpu.make_async_copy(u_ref, u, sems.at[2])

    def both(first, second):
        a = pltpu.make_async_copy(first, late, sems.at[0])
        b = pltpu.make_async_copy(second, early, sems.at[1])
        a.start()
        b.start()
        state.start()
        a.wait()
        b.wait()

    @pl.when(core == 1)
    def _():
        both(own_ref, other_ref)

    @pl.when(core == 0)
    def _():
        both(other_ref, own_ref)

    fill_weights(strip, class_ref, sets_ref, coef_ref)

    def split(value):
        big = value.astype(jnp.bfloat16)
        return big, (value - big.astype(jnp.float32)).astype(jnp.bfloat16)

    def times(a, b):
        return jnp.dot(a, b, preferred_element_type=jnp.float32)

    early_big, early_small = split(early[...])
    for part in range(2):
        rows = slice(part * HALF, (part + 1) * HALF)
        big, small = split(late[rows, :])
        q_ref[rows, :] = times(big, early_big) + (times(big, early_small) + times(small, early_big))
    half_ref[...] = q_ref[pl.ds(pl.multiple_of(core * HALF, HALF), HALF), :]
    cols = pl.ds(pl.multiple_of(strip // 2 * TILE, TILE), TILE)
    wide = jnp.where(core == 1, late[:, cols], q_ref[:, cols])
    turned = jnp.transpose(wide)
    columns[0:LOCAL, :] = jnp.where(lax.rem(strip, 2) == 1, turned[LOCAL:], turned[:LOCAL])
    state.wait()
    for k in range(TILES):
        cols = slice(k * TILE, (k + 1) * TILE)
        for br in range(2):
            part = u[br * BLK : (br + 1) * BLK, cols]
            sums_ref[br * TILES + k : br * TILES + k + 1, :] = jnp.sum(part, axis=0, keepdims=True)
    columns[LOCAL:, :] = jnp.zeros((8, COARSE), jnp.float32)
    columns[LOCAL:, 0:TILE] = jnp.broadcast_to(packed_means(sums_ref[...]), (8, TILE))
    done = pltpu.make_async_copy(columns, columns_ref, sems.at[0])
    done.start()
    done.wait()


def pair_product(tile_class, coeff_sets, own, other, state):
    square = pltpu.VMEM((COARSE, COARSE), jnp.float32)
    return pl.pallas_call(
        pair_kernel,
        cost_estimate=cost(3),
        out_shape=(
            jax.ShapeDtypeStruct((COARSE, COARSE), jnp.float32),
            jax.ShapeDtypeStruct((HALF, COARSE), jnp.float32),
            pltpu.HBM((LOCAL + 8, COARSE), jnp.float32),
            jax.ShapeDtypeStruct((TILES, 15, 8, TILE), jnp.float32),
        ),
        in_specs=[SMEM, SMEM, HBM, ANY, HBM],
        out_specs=(VMEM, VMEM, HBM, VMEM),
        scratch_shapes=[
            square,
            square,
            pltpu.VMEM((ROWS, COLS), jnp.float32),
            pltpu.VMEM((32, TILE), jnp.float32),
            pltpu.VMEM((LOCAL + 8, COARSE), jnp.float32),
            pltpu.SemaphoreType.DMA((3,)),
        ],
        compiler_params=pltpu.CompilerParams(vmem_limit_bytes=24 << 20),
    )(*in_hbm(tile_class, coeff_sets, own), other, *in_hbm(state))


def fine_kernel(corrected, coef, *refs):
    if corrected:
        c_ref, means_ref, own_ref, other_ref, own_columns_ref, columns_ref, *refs = refs
        up_ref, u_ref, down_ref, f_ref, fin_ref, out_ref, *refs = refs
        block, means_scratch, columns_scratch, extra, u_ext, first, second, force, sums_ref, sems = refs
        fields = [
            pltpu.make_async_copy(u_ref, u_ext.at[:, pl.ds(STEPS, ROWS)], extra.at[0]),
            pltpu.make_async_copy(f_ref, force, extra.at[1]),
        ]
        needed = [
            pltpu.make_async_copy(means_ref, means_scratch, extra.at[2]),
            pltpu.make_async_copy(own_columns_ref, columns_scratch, extra.at[3]),
        ]
        for copy in fields + needed:
            copy.start()
    else:
        up_ref, u_ref, f_ref, down_ref, fin_ref, out_ref, top_ref, bottom_ref, means_ref, force_ref, *refs = refs
        means_scratch, f_ext, f_sems, u_ext, first, second, force, sums_ref, sems = refs
        copies = []
        for k in range(TILES):
            cols = pl.ds(k * TILE, TILE)
            inner = pl.ds(STEPS, ROWS)
            copies.append(
                (
                    pltpu.make_async_copy(u_ref.at[:, cols], u_ext.at[k, inner], sems.at[k]),
                    pltpu.make_async_copy(f_ref.at[:, cols], f_ext.at[k, inner], f_sems.at[k]),
                )
            )
            for copy in copies[k]:
                copy.start()
    strip, core, _, _ = position()
    sub = iota((8, TILE), 0)
    lane = iota((8, TILE), 1)
    for k in range(TILES):
        cols = slice(k * TILE, (k + 1) * TILE)
        u_ext[k, 0:STEPS, :] = up_ref[0:STEPS, cols]
        u_ext[k, STEPS + ROWS : EXT, :] = down_ref[0:STEPS, cols]
        if not corrected:
            f_ext[k, 0:STEPS, :] = up_ref[STEPS : 2 * STEPS, cols]
            f_ext[k, STEPS + ROWS : EXT, :] = down_ref[STEPS : 2 * STEPS, cols]
    if corrected:
        for copy in fields:
            copy.wait()
    for k in range(TILES):
        if corrected:
            added = []
            for line in range(4):
                at = lax.rem(2 * strip + 15 + line, 16) * 32 + 2 * k
                added.append(jnp.where(lane < BLK, c_ref[0, at], c_ref[0, at + 1]))
        else:
            for copy in copies[k]:
                copy.wait()
        for i in range(LINES):
            rows = pl.ds(i * 8, 8)
            value = u_ext[k, pl.ds(i, 8, stride=LINES), :]
            if corrected:
                row = sub * LINES + i
                addend = jnp.where(row < STEPS + BLK, added[1], added[2])
                if i < STEPS:
                    addend = jnp.where(sub == 0, added[0], addend)
                if i >= LINES - STEPS:
                    addend = jnp.where(sub == 7, added[3], addend)
                value = value + addend
            else:
                force[k, rows, :] = STEP * f_ext[k, pl.ds(i, 8, stride=LINES), :]
            first[k, rows, :] = value
    results = []
    if not corrected:
        results.append(pltpu.make_async_copy(force, force_ref, f_sems.at[0]))
        results[0].start()

    def tile_step(old, new, k, last=False):
        before = lax.rem(k + TILES - 1, TILES)
        after = lax.rem(k + 1, TILES)
        line = [old[k, pl.ds(i * 8, 8), :] for i in range(LINES)]
        top = pltpu.roll(line[-1], 1, 0)
        bottom = pltpu.roll(line[0], 7, 0)
        for i in range(LINES):
            kind = (i < STEPS) + 2 * (i >= LINES - STEPS)
            centre, w_left, w_right, w_above, w_below = (coef[k, 5 * kind + w] for w in range(5))
            rows = pl.ds(i * 8, 8)
            left = pltpu.roll(jnp.where(lane == TILE - 1, old[before, rows, :], line[i]), 1, 1)
            right = pltpu.roll(jnp.where(lane == 0, old[after, rows, :], line[i]), TILE - 1, 1)
            above = line[i - 1] if i else top
            below = line[i + 1] if i + 1 < LINES else bottom
            new[k, pl.ds(i, 8, stride=LINES) if last else rows, :] = (
                (centre * line[i] + force[k, rows, :])
                + (w_left * left + w_right * right)
                + (w_above * above + w_below * below)
            )

    def sweep(old, new):
        def one_tile(k, carry):
            tile_step(old, new, k)
            return carry

        lax.fori_loop(0, TILES, one_tile, 0, unroll=16)

    def two_steps(_, carry):
        sweep(first, second)
        sweep(second, first)
        return carry

    lax.fori_loop(0, STEPS // 2 - 1, two_steps, 0)
    sweep(first, second)

    def last_tile(k, carry):
        tile_step(second, u_ext, k, last=True)
        for br in range(2):
            part = u_ext[k, STEPS + br * BLK : STEPS + (br + 1) * BLK, :]
            sums_ref[pl.ds(br * TILES + k, 1), :] = jnp.sum(part, axis=0, keepdims=True)
        return carry

    for part in range(2):
        half = TILES // 2
        tiles = pl.ds(part * half, half)
        lax.fori_loop(part * half, (part + 1) * half, last_tile, 0, unroll=8)
        copy = pltpu.make_async_copy(u_ext.at[tiles, pl.ds(STEPS, ROWS)], fin_ref.at[tiles], sems.at[part])
        copy.start()
        results.append(copy)
    if not corrected:
        for k in range(TILES):
            cols = slice(k * TILE, (k + 1) * TILE)
            top_ref[:, cols] = u_ext[k, STEPS : 2 * STEPS, :]
            bottom_ref[:, cols] = u_ext[k, ROWS : STEPS + ROWS, :]
    means = packed_means(sums_ref[...])
    if corrected:
        for copy in needed:
            copy.wait()
        grown = means - means_scratch[...]
        even = core == 0
        pushed = rows_times(grown - jnp.where(even, other_ref[...], 0.0), columns_ref[0:LOCAL, :])
        pushed = pushed - rows_times(jnp.where(even, own_ref[...], 0.0), columns_scratch[0:LOCAL, :])
        write_message(strip, pushed, grown, block, out_ref)
    else:
        out_ref[...] = means
        means_scratch[...] = means
        copy = pltpu.make_async_copy(means_scratch, means_ref, f_sems.at[1])
        copy.start()
        results.append(copy)
    for copy in results:
        copy.wait()


FIELD = pltpu.VMEM((TILES, EXT, TILE), jnp.float32)
EDGE = jax.ShapeDtypeStruct((STEPS, COLS), jnp.float32)


def fine_call(corrected, in_specs, more_out, more_specs, scratch, args):
    return pl.pallas_call(
        functools.partial(fine_kernel, corrected),
        cost_estimate=cost(10),
        out_shape=(pltpu.HBM((TILES, ROWS, TILE), jnp.float32), *more_out),
        in_specs=in_specs,
        out_specs=(HBM, *more_specs),
        scratch_shapes=[
            *scratch,
            FIELD,
            FIELD,
            FIELD,
            FIELD,
            pltpu.VMEM((32, TILE), jnp.float32),
            pltpu.SemaphoreType.DMA((TILES,)),
        ],
        compiler_params=pltpu.CompilerParams(vmem_limit_bytes=16 << 20),
    )(*args)


def first_sweep(coef, upper, state, source, lower):
    state, source = in_hbm(state, source)
    return fine_call(
        False,
        [VMEM, VMEM, HBM, HBM, VMEM],
        (
            jax.ShapeDtypeStruct((1, TILE), jnp.float32),
            EDGE,
            EDGE,
            pltpu.HBM((1, TILE), jnp.float32),
            pltpu.HBM((TILES, EXT, TILE), jnp.float32),
        ),
        (VMEM, VMEM, VMEM, HBM, HBM),
        [pltpu.VMEM((1, TILE), jnp.float32), FIELD, pltpu.SemaphoreType.DMA((TILES,))],
        (coef, upper, state, source, lower),
    )


def second_sweep(coef, correction, means, own_part, other_part, columns, next_columns, state, forcing):
    means, columns, forcing = in_hbm(means, columns, forcing)
    return fine_call(
        True,
        [VMEM, SMEM, HBM, VMEM, VMEM, HBM, VMEM, VMEM, ANY, VMEM, HBM],
        (jax.ShapeDtypeStruct((128 * PIECES, TILE), jnp.float32),),
        (VMEM,),
        [
            pltpu.VMEM((8 * PIECES, TILE), jnp.float32),
            pltpu.VMEM((1, TILE), jnp.float32),
            pltpu.VMEM((LOCAL + 8, COARSE), jnp.float32),
            pltpu.SemaphoreType.DMA((4,)),
        ],
        (coef, correction, means, own_part, other_part, columns, next_columns, *state, forcing),
    )


def rows_times(row, matrix):
    row = jnp.broadcast_to(row, (8, TILE))[:, :LOCAL]
    return jnp.dot(row, matrix, precision=HIGHEST, preferred_element_type=jnp.float32)


def write_message(strip, pushed, raw, block, out_ref):
    lane = iota((1, TILE), 1)
    raw = jnp.where((lane >= LOCAL) == (lax.rem(strip, 2) == 1), raw, 0.0)
    pieces = [pushed[0:1, q * TILE : (q + 1) * TILE] for q in range(4)] + [raw]
    for n in range(8):
        for q in range(PIECES):
            block[n * PIECES + q : n * PIECES + q + 1, :] = pieces[q]
    for n in range(16):
        out_ref[n * 8 * PIECES : (n + 1) * 8 * PIECES, :] = block[...]


def message_kernel(means_ref, base_ref, columns_ref, out_ref, block):
    defect = means_ref[...] - base_ref[...]
    strip, _, _, _ = position()
    write_message(strip, rows_times(defect, columns_ref[0:LOCAL, :]), defect, block, out_ref)


def message(means, base, columns):
    return pl.pallas_call(
        message_kernel,
        cost_estimate=cost(1),
        out_shape=jax.ShapeDtypeStruct((128 * PIECES, TILE), jnp.float32),
        in_specs=[VMEM, VMEM, VMEM],
        out_specs=VMEM,
        scratch_shapes=[pltpu.VMEM((8 * PIECES, TILE), jnp.float32)],
        compiler_params=pltpu.CompilerParams(vmem_limit_bytes=16 << 20),
    )(means, base, columns)


def add(a, b):
    return [p + q for p, q in zip(a, b, strict=True)]


def minus(a, b):
    return [p - q for p, q in zip(a, b, strict=True)]


def select(condition, a, b):
    return [jnp.where(condition, p, q) for p, q in zip(a, b, strict=True)]


def quarters(row):
    return [row[:, q * TILE : (q + 1) * TILE] for q in range(4)]


def applied(matrix, vector):
    diagonal = iota((TILE, TILE), 0) == iota((TILE, TILE), 1)
    column = jnp.sum(matrix * jnp.concatenate(vector, axis=1), axis=1, keepdims=True)
    return [
        jnp.sum(jnp.where(diagonal, column[q * TILE : (q + 1) * TILE], 0.0), axis=0, keepdims=True) for q in range(4)
    ]


def pushes(got_ref, window):
    start = lax.rem(window + 16, 16) * (8 * PIECES)
    return [jnp.sum(got_ref[pl.ds(start + q, 8, stride=PIECES), :], axis=0, keepdims=True) for q in range(4)]


def gathered(got_ref, window):
    start = lax.rem(window + 16, 16) * (8 * PIECES) + 4
    raw = got_ref[pl.ds(start, 8, stride=PIECES), :]
    return [raw[2 * q : 2 * q + 1] + raw[2 * q + 1 : 2 * q + 2] for q in range(4)]


def pair_pushes(got_ref, pair):
    at = 2 * lax.rem(pair, 8)
    return add(pushes(got_ref, at - 1), pushes(got_ref, at))


def strip_piece(strip, value):
    piece = value[3]
    for q in range(3):
        piece = jnp.where(strip // 2 == q, value[q], piece)
    return jnp.broadcast_to(piece, (8, TILE))


def first_chain_kernel(got_ref, other_ref, *refs):
    whole, halved = refs[:5], refs[5:11]
    out_ref, maps_ref, maps, sems, out_sems = refs[11:]
    strip, core, chip, y = position()

    def fetch(slot, source):
        for part in range(2):
            rows = pl.ds(part * HALF, HALF)
            pltpu.make_async_copy(source.at[rows], maps.at[slot, rows], sems.at[slot, part]).start()

    def fetch_halves(slot, which):
        for part, at in ((0, core), (1, 1 - core)):
            rows = pl.ds(pl.multiple_of(at * HALF, HALF), HALF)
            pltpu.make_async_copy(halved[2 * which + part], maps.at[slot, rows], sems.at[slot, part]).start()

    def fetch_turned(slot, pair, below):
        own = (core == 0) == below

        @pl.when(own)
        def _():
            fetch(slot, pair[0])

        @pl.when(jnp.logical_not(own))
        def _():
            fetch(slot, pair[1])

    def fetch_near(slot, ahead):
        if ahead == 2:
            fetch_halves(slot, 0)
        else:
            fetch_turned(slot, whole[0:2], ahead == 3)

    def fetch_far(slot, ahead):
        if ahead in (0, 2):
            fetch_halves(slot, 2 if ahead else 1)
        else:
            fetch_turned(slot, whole[2:4], ahead == 3)

    def landed(slot):
        for part in range(2):
            rows = pl.ds(0, HALF)
            pltpu.make_async_copy(whole[4].at[rows], maps.at[slot, rows], sems.at[slot, part]).wait()
        kept(slot).start()

    def kept(slot):
        return pltpu.make_async_copy(maps.at[slot], maps_ref.at[slot], out_sems.at[slot])

    for half in range(2):
        if half == 1:
            fetch_far(4, 0)
        for ahead in range(1, 4):
            wraps = y + ahead >= 4

            @pl.when(wraps == (half == 0))
            def _():
                fetch_far(4 * half + ahead, ahead)

            @pl.when(wraps != (half == 0))
            def _():
                fetch_near(4 * half + ahead, ahead)

    fetch(0, whole[4])
    fetch(8, other_ref)
    value = select(core == 1, pushes(got_ref, 2 * chip), pair_pushes(got_ref, chip))

    def arriving(step, value):
        landed(step)
        return add(applied(maps[step], value), pair_pushes(got_ref, chip + step))

    value = lax.fori_loop(1, 8, arriving, value)
    landed(0)
    landed(8)

    def again(step, value):
        return add(applied(maps[step], value), pair_pushes(got_ref, chip + step))

    value = lax.fori_loop(0, 8, again, value)
    value = select(core == 1, applied(maps[8], add(value, gathered(got_ref, 2 * chip + 15))), value)
    piece = strip_piece(strip, value)
    lane = iota((8, TILE), 1)
    here = jnp.where((lane < LOCAL) == (lax.rem(strip, 2) == 0), piece, pltpu.roll(piece, LOCAL, 1))
    out_ref[...] = jnp.concatenate(value + [here[0:1]], axis=1)
    for slot in range(9):
        kept(slot).wait()


def first_chain(got, other, whole, halved):
    whole[4], halved[2] = in_hbm(whole[4], halved[2])
    return pl.pallas_call(
        first_chain_kernel,
        cost_estimate=cost(5),
        out_shape=(
            jax.ShapeDtypeStruct((1, COARSE + TILE), jnp.float32),
            pltpu.HBM((9, COARSE, COARSE), jnp.float32),
        ),
        in_specs=[VMEM] + [ANY] * 12,
        out_specs=(VMEM, HBM),
        scratch_shapes=[
            pltpu.VMEM((9, COARSE, COARSE), jnp.float32),
            pltpu.SemaphoreType.DMA((9, 2)),
            pltpu.SemaphoreType.DMA((9,)),
        ],
        compiler_params=pltpu.CompilerParams(vmem_limit_bytes=16 << 20),
    )(got, other, *whole, *halved)


def last_chain_kernel(got_ref, own_ref, partner_ref, late_ref, maps_ref, u_ref, out_ref, late, maps, sems, u, whole, sem, out_sems):
    strip, core, chip, _ = position()

    def fetched(slot):
        return pltpu.make_async_copy(maps_ref.at[slot], maps.at[slot], sems.at[slot])

    first = pltpu.make_async_copy(late_ref, late, sems.at[9])
    first.start()
    for slot in (1, 2, 3, 4, 5, 6, 7, 0, 8):
        fetched(slot).start()
    state = pltpu.make_async_copy(u_ref, u, sem)
    state.start()
    own, partner = quarters(own_ref[...]), quarters(partner_ref[...])
    even_start = pair_pushes(got_ref, chip)
    odd_start = minus(gathered(got_ref, 2 * chip), own)
    first.wait()
    value = select(core == 1, applied(late[...], odd_start), even_start)

    def arriving(step, value):
        fetched(step).wait()
        return add(applied(maps[step], value), pair_pushes(got_ref, chip + step))

    value = lax.fori_loop(1, 8, arriving, value)
    fetched(0).wait()

    def again(step, value):
        return add(applied(maps[step], value), pair_pushes(got_ref, chip + step))

    value = lax.fori_loop(0, 8, again, value)
    fetched(8).wait()
    final = applied(maps[8], add(value, minus(gathered(got_ref, 2 * chip + 15), partner)))
    piece = strip_piece(strip, select(core == 1, final, value))
    state.wait()
    lane = iota((8, TILE), 1)
    outs = []
    for k in range(TILES):
        cols = slice(k * TILE, (k + 1) * TILE)
        for br in range(2):
            at = lax.rem(strip, 2) * LOCAL + br * 32 + 2 * k
            added = jnp.take_along_axis(piece, at + jnp.where(lane < BLK, 0, 1), axis=1)
            for n in range(BLK // 8):
                rows = slice(br * BLK + n * 8, br * BLK + (n + 1) * 8)
                whole[rows, cols] = u[k, rows, :] + added
        if k % 4 == 3:
            cols = pl.ds((k - 3) * TILE, 4 * TILE)
            copy = pltpu.make_async_copy(whole.at[:, cols], out_ref.at[:, cols], out_sems.at[k // 4])
            copy.start()
            outs.append(copy)
    for copy in outs:
        copy.wait()


def last_chain(got, own, partner, late, maps, previous):
    square = (COARSE, COARSE)
    return pl.pallas_call(
        last_chain_kernel,
        cost_estimate=cost(6),
        out_shape=jax.ShapeDtypeStruct((ROWS, COLS), jnp.float32),
        in_specs=[VMEM, VMEM, VMEM, HBM, HBM, ANY],
        out_specs=HBM,
        scratch_shapes=[
            pltpu.VMEM(square, jnp.float32),
            pltpu.VMEM((9, *square), jnp.float32),
            pltpu.SemaphoreType.DMA((10,)),
            pltpu.VMEM((TILES, ROWS, TILE), jnp.float32),
            pltpu.VMEM((ROWS, COLS), jnp.float32),
            pltpu.SemaphoreType.DMA,
            pltpu.SemaphoreType.DMA((4,)),
        ],
        compiler_params=pltpu.CompilerParams(vmem_limit_bytes=16 << 20),
    )(got, own, partner, *in_hbm(late, maps), previous)


def exchanged(block):
    block = block.reshape(128, 1, PIECES * TILE)
    return lax.all_to_all(block, ("tm", "space"), 0, 0, tiled=True).reshape(128 * PIECES, TILE)


def swapped(value):
    return moved(value, lambda x, y, z, core: (x, y, z, 1 - core))


def across(value):
    return moved(value, lambda x, y, z, core: (x, y, z + 1 - 2 * core, core))


def along(value, dz=0):
    return moved(value, lambda x, y, z, core: (x, y + 1 - 2 * core, z + dz * (1 - 2 * core), core))


def per_device(initial_states, sources, tile_class, coeff_sets, coarse_maps):
    state, source, own_map = initial_states[0], sources[0], coarse_maps[0]
    core = lax.axis_index("tm") % 2
    other_map = swapped(own_map)
    upper = shifted(jnp.concatenate([state[-STEPS:], source[-STEPS:]], axis=0), 0, 1)
    lower = shifted(jnp.concatenate([state[:STEPS], source[:STEPS]], axis=0), 0, -1)

    product, half, columns, coef = pair_product(tile_class, coeff_sets, own_map, other_map, state)
    product, half, columns, upper, lower = lax.optimization_barrier((product, half, columns, upper, lower))
    near = along(product)
    far_same = across(half)
    next_columns = shifted(columns, -1)

    finished, means, top, bottom, kept_means, forcing = first_sweep(coef, upper, state, source, lower)
    near, far_same, next_columns, means, finished = lax.optimization_barrier(
        (near, far_same, next_columns, means, finished)
    )
    near_half = lax.dynamic_slice(near, (core * HALF, 0), (HALF, COARSE))
    far = across(near)
    near_second = along(near_half)
    far_second = along(near_half, 1)

    got = exchanged(message(means, next_columns[LOCAL : LOCAL + 1, :TILE], next_columns))

    got, far, near_second, far_second, finished, top, bottom = lax.optimization_barrier(
        (got, far, near_second, far_second, finished, top, bottom)
    )
    previous = shifted(bottom, 1, 1), shifted(finished, 1), shifted(top, 1, -1)
    whole = [near, swapped(near), far, swapped(far), product]
    halved = []
    for part in (near_second, far_same, far_second):
        halved += [part, swapped(part)]
    correction, maps = first_chain(got, other_map, whole, halved)
    partner = swapped(correction)
    here, there = correction[:, :COARSE], partner[:, :COARSE]
    own_part, other_part = correction[:, COARSE:], partner[:, COARSE:]

    finished, block = second_sweep(
        coef, here, kept_means, own_part, other_part, columns, next_columns, previous, forcing
    )
    previous = shifted(finished, 1)
    got = exchanged(block)
    return last_chain(got, here, there, own_map, maps, previous)[None]


def solution(mesh):
    placed = (P("tm", "space", None), P("tm", "space", None), P(), P(), P("tm", None, None))
    return jax.shard_map(
        per_device, mesh=mesh, in_specs=placed, out_specs=P("tm", "space", None), check_vma=False
    )
```

```python
import functools

import jax
import jax.numpy as jnp
from jax import lax
from jax.experimental import pallas as pl
from jax.experimental.pallas import tpu as pltpu
from jax.sharding import PartitionSpec as P

TILE = 128
BLK = 64
STEPS = 8
ROWS = 128
COLS = 2048
COARSE = 512
HALF = COARSE // 2
TILES = COLS // TILE
EXT = ROWS + 2 * STEPS
LINES = EXT // 8
PARTS = 4
LOCAL = 64
PIECES = 5
STEP = 0.6

HIGHEST = lax.Precision.HIGHEST
HBM = pl.BlockSpec(memory_space=pltpu.HBM)
ANY = pl.BlockSpec(memory_space=pl.ANY)
SMEM = pl.BlockSpec(memory_space=pltpu.SMEM)
VMEM = pl.BlockSpec(memory_space=pltpu.VMEM)


def place(device):
    tm, space = divmod(device, 8)
    z_lo, rest = divmod(tm, 8)
    y, core = divmod(rest, 2)
    z_hi, x = divmod(space, 4)
    return x, y, 2 * z_hi + z_lo, core


def device_at(x, y, z, core):
    x, y, z, core = x % 4, y % 4, z % 4, core % 2
    return ((z % 2) * 8 + y * 2 + core) * 8 + (z // 2) * 4 + x


def moved(value, route):
    pairs = [(i, device_at(*route(*place(i)))) for i in range(128)]
    return lax.ppermute(value, ("tm", "space"), pairs)


def shifted(value, windows, strips=0):
    pairs = [
        (tm * 8 + sp, (tm + windows) % 16 * 8 + (sp + strips) % 8)
        for tm in range(16)
        for sp in range(8)
    ]
    return lax.ppermute(value, ("tm", "space"), pairs)


def cost(micros):
    return pl.CostEstimate(flops=0, transcendentals=0, bytes_accessed=int(micros * 3.6e6))


def in_hbm(*values):
    return [pltpu.with_memory_space_constraint(value, pltpu.HBM) for value in values]


def position():
    window = lax.axis_index("tm")
    pair = window // 2
    return lax.axis_index("space"), lax.rem(window, 2), pair, lax.rem(pair, 4)


def iota(shape, axis):
    return lax.broadcasted_iota(jnp.int32, shape, axis)


def packed_means(sums):
    lane = iota((32, TILE), 1)
    row = iota((32, TILE), 0)
    low = jnp.sum(jnp.where(lane < BLK, sums, 0.0), axis=1, keepdims=True)
    high = jnp.sum(jnp.where(lane < BLK, 0.0, sums), axis=1, keepdims=True)
    slot = lane & (LOCAL - 1)
    spread = jnp.where(slot == 2 * row, low, 0.0) + jnp.where(slot == 2 * row + 1, high, 0.0)
    return jnp.sum(spread, axis=0, keepdims=True) * (1.0 / (BLK * BLK))


def fill_weights(strip, class_ref, sets_ref, coef_ref):
    sub = iota((8, TILE), 0)
    strips = (lax.rem(strip + 7, 8), strip, lax.rem(strip + 1, 8))

    def weights(row, k):
        label = class_ref[row, k]
        spread, along_cols, along_rows = sets_ref[0, label], sets_ref[1, label], sets_ref[2, label]
        left = STEP * (spread + jnp.maximum(along_cols, 0.0))
        right = STEP * (spread - jnp.minimum(along_cols, 0.0))
        above = STEP * (spread + jnp.maximum(along_rows, 0.0))
        below = STEP * (spread - jnp.minimum(along_rows, 0.0))
        return 1.0 - (left + right + above + below), left, right, above, below

    for k in range(TILES):
        upper, inner, lower = (weights(row, k) for row in strips)
        for w in range(5):
            value = jnp.full((8, TILE), inner[w], jnp.float32)
            coef_ref[k, w] = value
            coef_ref[k, 5 + w] = jnp.where(sub == 0, upper[w], value)
            coef_ref[k, 10 + w] = jnp.where(sub == 7, lower[w], value)


def pair_kernel(class_ref, sets_ref, own_ref, other_ref, u_ref, q_ref, half_ref, columns_ref, coef_ref, *scratch):
    late, early, u, sums_ref, columns, sems = scratch
    strip, core, _, _ = position()
    state = pltpu.make_async_copy(u_ref, u, sems.at[2])

    def both(first, second):
        a = pltpu.make_async_copy(first, late, sems.at[0])
        b = pltpu.make_async_copy(second, early, sems.at[1])
        a.start()
        b.start()
        state.start()
        a.wait()
        b.wait()

    @pl.when(core == 1)
    def _():
        both(own_ref, other_ref)

    @pl.when(core == 0)
    def _():
        both(other_ref, own_ref)

    fill_weights(strip, class_ref, sets_ref, coef_ref)

    def split(value):
        big = value.astype(jnp.bfloat16)
        return big, (value - big.astype(jnp.float32)).astype(jnp.bfloat16)

    def times(a, b):
        return jnp.dot(a, b, preferred_element_type=jnp.float32)

    early_big, early_small = split(early[...])
    for part in range(2):
        rows = slice(part * HALF, (part + 1) * HALF)
        big, small = split(late[rows, :])
        q_ref[rows, :] = times(big, early_big) + (times(big, early_small) + times(small, early_big))
    half_ref[...] = q_ref[pl.ds(pl.multiple_of(core * HALF, HALF), HALF), :]
    cols = pl.ds(pl.multiple_of(strip // 2 * TILE, TILE), TILE)
    wide = jnp.where(core == 1, late[:, cols], q_ref[:, cols])
    turned = jnp.transpose(wide)
    columns[0:LOCAL, :] = jnp.where(lax.rem(strip, 2) == 1, turned[LOCAL:], turned[:LOCAL])
    state.wait()
    for k in range(TILES):
        cols = slice(k * TILE, (k + 1) * TILE)
        for br in range(2):
            part = u[br * BLK : (br + 1) * BLK, cols]
            sums_ref[br * TILES + k : br * TILES + k + 1, :] = jnp.sum(part, axis=0, keepdims=True)
    columns[LOCAL:, :] = jnp.zeros((8, COARSE), jnp.float32)
    columns[LOCAL:, 0:TILE] = jnp.broadcast_to(packed_means(sums_ref[...]), (8, TILE))
    done = pltpu.make_async_copy(columns, columns_ref, sems.at[0])
    done.start()
    done.wait()


def pair_product(tile_class, coeff_sets, own, other, state):
    square = pltpu.VMEM((COARSE, COARSE), jnp.float32)
    return pl.pallas_call(
        pair_kernel,
        cost_estimate=cost(3),
        out_shape=(
            jax.ShapeDtypeStruct((COARSE, COARSE), jnp.float32),
            jax.ShapeDtypeStruct((HALF, COARSE), jnp.float32),
            pltpu.HBM((LOCAL + 8, COARSE), jnp.float32),
            jax.ShapeDtypeStruct((TILES, 15, 8, TILE), jnp.float32),
        ),
        in_specs=[SMEM, SMEM, HBM, ANY, HBM],
        out_specs=(VMEM, VMEM, HBM, VMEM),
        scratch_shapes=[
            square,
            square,
            pltpu.VMEM((ROWS, COLS), jnp.float32),
            pltpu.VMEM((32, TILE), jnp.float32),
            pltpu.VMEM((LOCAL + 8, COARSE), jnp.float32),
            pltpu.SemaphoreType.DMA((3,)),
        ],
        compiler_params=pltpu.CompilerParams(vmem_limit_bytes=24 << 20),
    )(*in_hbm(tile_class, coeff_sets, own), other, *in_hbm(state))


def fine_kernel(corrected, coef, *refs):
    if corrected:
        c_ref, means_ref, own_ref, other_ref, own_columns_ref, columns_ref, *refs = refs
        up_ref, u_ref, down_ref, f_ref, fin_ref, out_ref, *refs = refs
        block, means_scratch, columns_scratch, extra, u_ext, first, second, force, sums_ref, sems = refs
        states, forces = [], []
        for n in range(PARTS):
            tiles = pl.ds(n * TILES // PARTS, TILES // PARTS)
            states.append(pltpu.make_async_copy(u_ref.at[tiles], u_ext.at[tiles, pl.ds(STEPS, ROWS)], sems.at[n]))
            forces.append(pltpu.make_async_copy(f_ref.at[tiles], force.at[tiles], sems.at[PARTS + n]))
        needed = [
            pltpu.make_async_copy(means_ref, means_scratch, extra.at[0]),
            pltpu.make_async_copy(own_columns_ref, columns_scratch, extra.at[1]),
        ]
        for copy in states + forces + needed:
            copy.start()
    else:
        up_ref, u_ref, f_ref, down_ref, fin_ref, out_ref, top_ref, bottom_ref, means_ref, force_ref, *refs = refs
        means_scratch, f_ext, f_sems, u_ext, first, second, force, sums_ref, sems = refs
        copies = []
        for k in range(TILES):
            cols = pl.ds(k * TILE, TILE)
            inner = pl.ds(STEPS, ROWS)
            copies.append(
                (
                    pltpu.make_async_copy(u_ref.at[:, cols], u_ext.at[k, inner], sems.at[k]),
                    pltpu.make_async_copy(f_ref.at[:, cols], f_ext.at[k, inner], f_sems.at[k]),
                )
            )
            for copy in copies[k]:
                copy.start()
    strip, core, _, _ = position()
    sub = iota((8, TILE), 0)
    lane = iota((8, TILE), 1)
    for k in range(TILES):
        cols = slice(k * TILE, (k + 1) * TILE)
        u_ext[k, 0:STEPS, :] = up_ref[0:STEPS, cols]
        u_ext[k, STEPS + ROWS : EXT, :] = down_ref[0:STEPS, cols]
        if not corrected:
            f_ext[k, 0:STEPS, :] = up_ref[STEPS : 2 * STEPS, cols]
            f_ext[k, STEPS + ROWS : EXT, :] = down_ref[STEPS : 2 * STEPS, cols]
    quarter, places = [], []
    if corrected:
        for line in range(4):
            block_row = lax.rem(2 * strip + 15 + line, 16)
            cols = pl.ds(pl.multiple_of(block_row // 4 * TILE, TILE), TILE)
            quarter.append(jnp.broadcast_to(c_ref[:, cols], (8, TILE)))
            places.append(lax.rem(block_row, 4) * 32)
    for k in range(TILES):
        if corrected:
            if k % (TILES // PARTS) == 0:
                states[k * PARTS // TILES].wait()
            added = []
            for line in range(4):
                at = jnp.where(lane < BLK, 2 * k, 2 * k + 1) + places[line]
                added.append(jnp.take_along_axis(quarter[line], at, axis=1))
        else:
            for copy in copies[k]:
                copy.wait()
        for i in range(LINES):
            rows = pl.ds(i * 8, 8)
            value = u_ext[k, pl.ds(i, 8, stride=LINES), :]
            if corrected:
                row = sub * LINES + i
                addend = jnp.where(row < STEPS + BLK, added[1], added[2])
                if i < STEPS:
                    addend = jnp.where(sub == 0, added[0], addend)
                if i >= LINES - STEPS:
                    addend = jnp.where(sub == 7, added[3], addend)
                value = value + addend
            else:
                force[k, rows, :] = STEP * f_ext[k, pl.ds(i, 8, stride=LINES), :]
            first[k, rows, :] = value
    results = []
    if corrected:
        for copy in forces:
            copy.wait()
    else:
        results.append(pltpu.make_async_copy(force, force_ref, f_sems.at[0]))
        results[0].start()

    def tile_step(old, new, k, last=False):
        before = lax.rem(k + TILES - 1, TILES)
        after = lax.rem(k + 1, TILES)
        line = [old[k, pl.ds(i * 8, 8), :] for i in range(LINES)]
        top = pltpu.roll(line[-1], 1, 0)
        bottom = pltpu.roll(line[0], 7, 0)
        for i in range(LINES):
            kind = (i < STEPS) + 2 * (i >= LINES - STEPS)
            centre, w_left, w_right, w_above, w_below = (coef[k, 5 * kind + w] for w in range(5))
            rows = pl.ds(i * 8, 8)
            left = pltpu.roll(jnp.where(lane == TILE - 1, old[before, rows, :], line[i]), 1, 1)
            right = pltpu.roll(jnp.where(lane == 0, old[after, rows, :], line[i]), TILE - 1, 1)
            above = line[i - 1] if i else top
            below = line[i + 1] if i + 1 < LINES else bottom
            new[k, pl.ds(i, 8, stride=LINES) if last else rows, :] = (
                (centre * line[i] + force[k, rows, :])
                + (w_left * left + w_right * right)
                + (w_above * above + w_below * below)
            )

    def sweep(old, new):
        def one_tile(k, carry):
            tile_step(old, new, k)
            return carry

        lax.fori_loop(0, TILES, one_tile, 0, unroll=16)

    def two_steps(_, carry):
        sweep(first, second)
        sweep(second, first)
        return carry

    lax.fori_loop(0, STEPS // 2 - 1, two_steps, 0)
    sweep(first, second)

    def last_tile(k, carry):
        tile_step(second, u_ext, k, last=True)
        for br in range(2):
            part = u_ext[k, STEPS + br * BLK : STEPS + (br + 1) * BLK, :]
            sums_ref[pl.ds(br * TILES + k, 1), :] = jnp.sum(part, axis=0, keepdims=True)
        return carry

    for part in range(4):
        half = TILES // 4
        tiles = pl.ds(part * half, half)
        lax.fori_loop(part * half, (part + 1) * half, last_tile, 0, unroll=4)
        copy = pltpu.make_async_copy(u_ext.at[tiles, pl.ds(STEPS, ROWS)], fin_ref.at[tiles], sems.at[part])
        copy.start()
        results.append(copy)
    if not corrected:
        for k in range(TILES):
            cols = slice(k * TILE, (k + 1) * TILE)
            top_ref[:, cols] = u_ext[k, STEPS : 2 * STEPS, :]
            bottom_ref[:, cols] = u_ext[k, ROWS : STEPS + ROWS, :]
    means = packed_means(sums_ref[...])
    if corrected:
        for copy in needed:
            copy.wait()
        grown = means - means_scratch[...]
        even = core == 0
        pushed = rows_times(grown - jnp.where(even, other_ref[...], 0.0), columns_ref[0:LOCAL, :])
        pushed = pushed - rows_times(jnp.where(even, own_ref[...], 0.0), columns_scratch[0:LOCAL, :])
        write_message(strip, pushed, grown, block, out_ref)
    else:
        out_ref[...] = means
        means_scratch[...] = means
        copy = pltpu.make_async_copy(means_scratch, means_ref, f_sems.at[1])
        copy.start()
        results.append(copy)
    for copy in results:
        copy.wait()


FIELD = pltpu.VMEM((TILES, EXT, TILE), jnp.float32)
EDGE = jax.ShapeDtypeStruct((STEPS, COLS), jnp.float32)


def fine_call(corrected, in_specs, more_out, more_specs, scratch, args):
    return pl.pallas_call(
        functools.partial(fine_kernel, corrected),
        cost_estimate=cost(10),
        out_shape=(pltpu.HBM((TILES, ROWS, TILE), jnp.float32), *more_out),
        in_specs=in_specs,
        out_specs=(HBM, *more_specs),
        scratch_shapes=[
            *scratch,
            FIELD,
            FIELD,
            FIELD,
            FIELD,
            pltpu.VMEM((32, TILE), jnp.float32),
            pltpu.SemaphoreType.DMA((TILES,)),
        ],
        compiler_params=pltpu.CompilerParams(vmem_limit_bytes=16 << 20),
    )(*args)


def first_sweep(coef, upper, state, source, lower):
    state, source = in_hbm(state, source)
    return fine_call(
        False,
        [VMEM, VMEM, HBM, HBM, VMEM],
        (
            jax.ShapeDtypeStruct((1, TILE), jnp.float32),
            EDGE,
            EDGE,
            pltpu.HBM((1, TILE), jnp.float32),
            pltpu.HBM((TILES, EXT, TILE), jnp.float32),
        ),
        (VMEM, VMEM, VMEM, HBM, HBM),
        [pltpu.VMEM((1, TILE), jnp.float32), FIELD, pltpu.SemaphoreType.DMA((TILES,))],
        (coef, upper, state, source, lower),
    )


def second_sweep(coef, correction, means, own_part, other_part, columns, next_columns, state, forcing):
    means, columns, forcing = in_hbm(means, columns, forcing)
    return fine_call(
        True,
        [VMEM, VMEM, HBM, VMEM, VMEM, HBM, VMEM, VMEM, ANY, VMEM, HBM],
        (jax.ShapeDtypeStruct((128 * PIECES, TILE), jnp.float32),),
        (VMEM,),
        [
            pltpu.VMEM((8 * PIECES, TILE), jnp.float32),
            pltpu.VMEM((1, TILE), jnp.float32),
            pltpu.VMEM((LOCAL + 8, COARSE), jnp.float32),
            pltpu.SemaphoreType.DMA((2,)),
        ],
        (coef, correction, means, own_part, other_part, columns, next_columns, *state, forcing),
    )


def rows_times(row, matrix):
    row = jnp.broadcast_to(row, (8, TILE))[:, :LOCAL]
    return jnp.dot(row, matrix, precision=HIGHEST, preferred_element_type=jnp.float32)


def write_message(strip, pushed, raw, block, out_ref):
    lane = iota((1, TILE), 1)
    raw = jnp.where((lane >= LOCAL) == (lax.rem(strip, 2) == 1), raw, 0.0)
    pieces = [pushed[0:1, q * TILE : (q + 1) * TILE] for q in range(4)] + [raw]
    for n in range(8):
        for q in range(PIECES):
            block[n * PIECES + q : n * PIECES + q + 1, :] = pieces[q]
    for n in range(16):
        out_ref[n * 8 * PIECES : (n + 1) * 8 * PIECES, :] = block[...]


def message_kernel(means_ref, base_ref, columns_ref, out_ref, block, out, sem):
    defect = means_ref[...] - base_ref[...]
    strip, _, _, _ = position()
    write_message(strip, rows_times(defect, columns_ref[0:LOCAL, :]), defect, block, out)
    sent = pltpu.make_async_copy(out, out_ref, sem)
    sent.start()
    sent.wait()


def message(means, base, columns):
    return pl.pallas_call(
        message_kernel,
        cost_estimate=cost(1),
        out_shape=pltpu.HBM((128 * PIECES, TILE), jnp.float32),
        in_specs=[VMEM, VMEM, VMEM],
        out_specs=HBM,
        scratch_shapes=[
            pltpu.VMEM((8 * PIECES, TILE), jnp.float32),
            pltpu.VMEM((128 * PIECES, TILE), jnp.float32),
            pltpu.SemaphoreType.DMA,
        ],
        compiler_params=pltpu.CompilerParams(vmem_limit_bytes=16 << 20),
    )(means, base, columns)


def add(a, b):
    return [p + q for p, q in zip(a, b, strict=True)]


def minus(a, b):
    return [p - q for p, q in zip(a, b, strict=True)]


def select(condition, a, b):
    return [jnp.where(condition, p, q) for p, q in zip(a, b, strict=True)]


def quarters(row):
    return [row[:, q * TILE : (q + 1) * TILE] for q in range(4)]


def applied(matrix, vector):
    diagonal = iota((TILE, TILE), 0) == iota((TILE, TILE), 1)
    column = jnp.sum(matrix * jnp.concatenate(vector, axis=1), axis=1, keepdims=True)
    return [
        jnp.sum(jnp.where(diagonal, column[q * TILE : (q + 1) * TILE], 0.0), axis=0, keepdims=True) for q in range(4)
    ]


def pushes(got_ref, window):
    start = lax.rem(window + 16, 16) * (8 * PIECES)
    return [jnp.sum(got_ref[pl.ds(start + q, 8, stride=PIECES), :], axis=0, keepdims=True) for q in range(4)]


def gathered(got_ref, window):
    start = lax.rem(window + 16, 16) * (8 * PIECES) + 4
    raw = got_ref[pl.ds(start, 8, stride=PIECES), :]
    return [raw[2 * q : 2 * q + 1] + raw[2 * q + 1 : 2 * q + 2] for q in range(4)]


def pair_pushes(got_ref, pair):
    at = 2 * lax.rem(pair, 8)
    return add(pushes(got_ref, at - 1), pushes(got_ref, at))


def strip_piece(strip, value):
    piece = value[3]
    for q in range(3):
        piece = jnp.where(strip // 2 == q, value[q], piece)
    return jnp.broadcast_to(piece, (8, TILE))


def first_chain_kernel(got_ref, other_ref, *refs):
    whole, halved = refs[:5], refs[5:11]
    out_ref, maps_ref, maps, sems, out_sems = refs[11:]
    strip, core, chip, y = position()

    def fetch(slot, source):
        for part in range(2):
            rows = pl.ds(part * HALF, HALF)
            pltpu.make_async_copy(source.at[rows], maps.at[slot, rows], sems.at[slot, part]).start()

    def fetch_halves(slot, which):
        for part, at in ((0, core), (1, 1 - core)):
            rows = pl.ds(pl.multiple_of(at * HALF, HALF), HALF)
            pltpu.make_async_copy(halved[2 * which + part], maps.at[slot, rows], sems.at[slot, part]).start()

    def fetch_turned(slot, pair, below):
        own = (core == 0) == below

        @pl.when(own)
        def _():
            fetch(slot, pair[0])

        @pl.when(jnp.logical_not(own))
        def _():
            fetch(slot, pair[1])

    def fetch_near(slot, ahead):
        if ahead == 2:
            fetch_halves(slot, 0)
        else:
            fetch_turned(slot, whole[0:2], ahead == 3)

    def fetch_far(slot, ahead):
        if ahead in (0, 2):
            fetch_halves(slot, 2 if ahead else 1)
        else:
            fetch_turned(slot, whole[2:4], ahead == 3)

    def landed(slot):
        for part in range(2):
            rows = pl.ds(0, HALF)
            pltpu.make_async_copy(whole[4].at[rows], maps.at[slot, rows], sems.at[slot, part]).wait()
        kept(slot).start()

    def kept(slot):
        return pltpu.make_async_copy(maps.at[slot], maps_ref.at[slot], out_sems.at[slot])

    for half in range(2):
        if half == 1:
            fetch_far(4, 0)
        for ahead in range(1, 4):
            wraps = y + ahead >= 4

            @pl.when(wraps == (half == 0))
            def _():
                fetch_far(4 * half + ahead, ahead)

            @pl.when(wraps != (half == 0))
            def _():
                fetch_near(4 * half + ahead, ahead)

    fetch(0, whole[4])
    fetch(8, other_ref)
    value = select(core == 1, pushes(got_ref, 2 * chip), pair_pushes(got_ref, chip))

    def arriving(step, value):
        landed(step)
        return add(applied(maps[step], value), pair_pushes(got_ref, chip + step))

    value = lax.fori_loop(1, 8, arriving, value)
    landed(0)
    landed(8)

    def again(step, value):
        return add(applied(maps[step], value), pair_pushes(got_ref, chip + step))

    value = lax.fori_loop(0, 8, again, value)
    value = select(core == 1, applied(maps[8], add(value, gathered(got_ref, 2 * chip + 15))), value)
    piece = strip_piece(strip, value)
    lane = iota((8, TILE), 1)
    here = jnp.where((lane < LOCAL) == (lax.rem(strip, 2) == 0), piece, pltpu.roll(piece, LOCAL, 1))
    out_ref[...] = jnp.concatenate(value + [here[0:1]], axis=1)
    for slot in range(9):
        kept(slot).wait()


def first_chain(got, other, whole, halved):
    whole[4], halved[2] = in_hbm(whole[4], halved[2])
    return pl.pallas_call(
        first_chain_kernel,
        cost_estimate=cost(5),
        out_shape=(
            jax.ShapeDtypeStruct((1, COARSE + TILE), jnp.float32),
            pltpu.HBM((9, COARSE, COARSE), jnp.float32),
        ),
        in_specs=[VMEM] + [ANY] * 12,
        out_specs=(VMEM, HBM),
        scratch_shapes=[
            pltpu.VMEM((9, COARSE, COARSE), jnp.float32),
            pltpu.SemaphoreType.DMA((9, 2)),
            pltpu.SemaphoreType.DMA((9,)),
        ],
        compiler_params=pltpu.CompilerParams(vmem_limit_bytes=16 << 20),
    )(got, other, *whole, *halved)


def last_chain_kernel(got_ref, own_ref, partner_ref, late_ref, maps_ref, u_ref, out_ref, late, maps, sems, u, whole, sem, out_sems):
    strip, core, chip, _ = position()

    def fetched(slot):
        return pltpu.make_async_copy(maps_ref.at[slot], maps.at[slot], sems.at[slot])

    first = pltpu.make_async_copy(late_ref, late, sems.at[9])
    first.start()
    for slot in (1, 2, 3, 4, 5, 6, 7, 0, 8):
        fetched(slot).start()
    state = pltpu.make_async_copy(u_ref, u, sem)
    state.start()
    own, partner = quarters(own_ref[...]), quarters(partner_ref[...])
    even_start = pair_pushes(got_ref, chip)
    odd_start = minus(gathered(got_ref, 2 * chip), own)
    first.wait()
    value = select(core == 1, applied(late[...], odd_start), even_start)

    def arriving(step, value):
        fetched(step).wait()
        return add(applied(maps[step], value), pair_pushes(got_ref, chip + step))

    value = lax.fori_loop(1, 8, arriving, value)
    fetched(0).wait()

    def again(step, value):
        return add(applied(maps[step], value), pair_pushes(got_ref, chip + step))

    value = lax.fori_loop(0, 8, again, value)
    fetched(8).wait()
    final = applied(maps[8], add(value, minus(gathered(got_ref, 2 * chip + 15), partner)))
    piece = strip_piece(strip, select(core == 1, final, value))
    state.wait()
    lane = iota((8, TILE), 1)
    outs = []
    for k in range(TILES):
        cols = slice(k * TILE, (k + 1) * TILE)
        for br in range(2):
            at = lax.rem(strip, 2) * LOCAL + br * 32 + 2 * k
            added = jnp.take_along_axis(piece, at + jnp.where(lane < BLK, 0, 1), axis=1)
            for n in range(BLK // 8):
                rows = slice(br * BLK + n * 8, br * BLK + (n + 1) * 8)
                whole[rows, cols] = u[k, rows, :] + added
        if k % 4 == 3:
            cols = pl.ds((k - 3) * TILE, 4 * TILE)
            copy = pltpu.make_async_copy(whole.at[:, cols], out_ref.at[:, cols], out_sems.at[k // 4])
            copy.start()
            outs.append(copy)
    for copy in outs:
        copy.wait()


def last_chain(got, own, partner, late, maps, previous):
    square = (COARSE, COARSE)
    return pl.pallas_call(
        last_chain_kernel,
        cost_estimate=cost(6),
        out_shape=jax.ShapeDtypeStruct((ROWS, COLS), jnp.float32),
        in_specs=[VMEM, VMEM, VMEM, HBM, HBM, ANY],
        out_specs=HBM,
        scratch_shapes=[
            pltpu.VMEM(square, jnp.float32),
            pltpu.VMEM((9, *square), jnp.float32),
            pltpu.SemaphoreType.DMA((10,)),
            pltpu.VMEM((TILES, ROWS, TILE), jnp.float32),
            pltpu.VMEM((ROWS, COLS), jnp.float32),
            pltpu.SemaphoreType.DMA,
            pltpu.SemaphoreType.DMA((4,)),
        ],
        compiler_params=pltpu.CompilerParams(vmem_limit_bytes=16 << 20),
    )(got, own, partner, *in_hbm(late, maps), previous)


def exchanged(block):
    block = block.reshape(128, 1, PIECES * TILE)
    return lax.all_to_all(block, ("tm", "space"), 0, 0, tiled=True).reshape(128 * PIECES, TILE)


def swapped(value):
    return moved(value, lambda x, y, z, core: (x, y, z, 1 - core))


def across(value):
    return moved(value, lambda x, y, z, core: (x, y, z + 1 - 2 * core, core))


def along(value, dz=0):
    return moved(value, lambda x, y, z, core: (x, y + 1 - 2 * core, z + dz * (1 - 2 * core), core))


def per_device(initial_states, sources, tile_class, coeff_sets, coarse_maps):
    state, source, own_map = initial_states[0], sources[0], coarse_maps[0]
    core = lax.axis_index("tm") % 2
    other_map = swapped(own_map)
    upper = shifted(jnp.concatenate([state[-STEPS:], source[-STEPS:]], axis=0), 0, 1)
    lower = shifted(jnp.concatenate([state[:STEPS], source[:STEPS]], axis=0), 0, -1)

    product, half, columns, coef = pair_product(tile_class, coeff_sets, own_map, other_map, state)
    product, half, columns, upper, lower = lax.optimization_barrier((product, half, columns, upper, lower))
    near = along(product)
    far_same = across(half)
    next_columns = shifted(columns, -1)

    finished, means, top, bottom, kept_means, forcing = first_sweep(coef, upper, state, source, lower)
    block = message(means, next_columns[LOCAL : LOCAL + 1, :TILE], next_columns)
    near, far_same, next_columns, block, finished = lax.optimization_barrier(
        (near, far_same, next_columns, block, finished)
    )
    near_half = lax.dynamic_slice(near, (core * HALF, 0), (HALF, COARSE))
    far = across(near)
    near_second = along(near_half)
    far_second = along(near_half, 1)

    got = exchanged(block)

    got, far, near_second, far_second, finished, top, bottom = lax.optimization_barrier(
        (got, far, near_second, far_second, finished, top, bottom)
    )
    previous = shifted(bottom, 1, 1), shifted(finished, 1), shifted(top, 1, -1)
    whole = [near, swapped(near), far, swapped(far), product]
    halved = []
    for part in (near_second, far_same, far_second):
        halved += [part, swapped(part)]
    correction, maps = first_chain(got, other_map, whole, halved)
    partner = swapped(correction)
    here, there = correction[:, :COARSE], partner[:, :COARSE]
    own_part, other_part = correction[:, COARSE:], partner[:, COARSE:]

    finished, block = second_sweep(
        coef, here, kept_means, own_part, other_part, columns, next_columns, previous, forcing
    )
    previous = shifted(finished, 1)
    got = exchanged(block)
    return last_chain(got, here, there, own_map, maps, previous)[None]


def solution(mesh):
    placed = (P("tm", "space", None), P("tm", "space", None), P(), P(), P("tm", None, None))
    return jax.shard_map(
        per_device, mesh=mesh, in_specs=placed, out_specs=P("tm", "space", None), check_vma=False
    )
```

```python
import functools

import jax
import jax.numpy as jnp
from jax import lax
from jax.experimental import pallas as pl
from jax.experimental.pallas import tpu as pltpu
from jax.sharding import PartitionSpec as P

TILE = 128
BLK = 64
STEPS = 8
ROWS = 128
COLS = 2048
COARSE = 512
HALF = COARSE // 2
TILES = COLS // TILE
EXT = ROWS + 2 * STEPS
LINES = EXT // 8
PARTS = 4
LOCAL = 64
PIECES = 5
STEP = 0.6

HIGHEST = lax.Precision.HIGHEST
HBM = pl.BlockSpec(memory_space=pltpu.HBM)
ANY = pl.BlockSpec(memory_space=pl.ANY)
SMEM = pl.BlockSpec(memory_space=pltpu.SMEM)
VMEM = pl.BlockSpec(memory_space=pltpu.VMEM)


def place(device):
    tm, space = divmod(device, 8)
    z_lo, rest = divmod(tm, 8)
    y, core = divmod(rest, 2)
    z_hi, x = divmod(space, 4)
    return x, y, 2 * z_hi + z_lo, core


def device_at(x, y, z, core):
    x, y, z, core = x % 4, y % 4, z % 4, core % 2
    return ((z % 2) * 8 + y * 2 + core) * 8 + (z // 2) * 4 + x


def moved(value, route):
    pairs = [(i, device_at(*route(*place(i)))) for i in range(128)]
    return lax.ppermute(value, ("tm", "space"), pairs)


def shifted(value, windows, strips=0):
    pairs = [
        (tm * 8 + sp, (tm + windows) % 16 * 8 + (sp + strips) % 8)
        for tm in range(16)
        for sp in range(8)
    ]
    return lax.ppermute(value, ("tm", "space"), pairs)


def cost(micros):
    return pl.CostEstimate(flops=0, transcendentals=0, bytes_accessed=int(micros * 3.6e6))


def in_hbm(*values):
    return [pltpu.with_memory_space_constraint(value, pltpu.HBM) for value in values]


def position():
    window = lax.axis_index("tm")
    pair = window // 2
    return lax.axis_index("space"), lax.rem(window, 2), pair, lax.rem(pair, 4)


def iota(shape, axis):
    return lax.broadcasted_iota(jnp.int32, shape, axis)


def packed_means(sums):
    lane = iota((32, TILE), 1)
    row = iota((32, TILE), 0)
    low = jnp.sum(jnp.where(lane < BLK, sums, 0.0), axis=1, keepdims=True)
    high = jnp.sum(jnp.where(lane < BLK, 0.0, sums), axis=1, keepdims=True)
    slot = lane & (LOCAL - 1)
    spread = jnp.where(slot == 2 * row, low, 0.0) + jnp.where(slot == 2 * row + 1, high, 0.0)
    return jnp.sum(spread, axis=0, keepdims=True) * (1.0 / (BLK * BLK))


def fill_weights(strip, class_ref, sets_ref, coef_ref):
    sub = iota((8, TILE), 0)
    strips = (lax.rem(strip + 7, 8), strip, lax.rem(strip + 1, 8))

    def weights(row, k):
        label = class_ref[row, k]
        spread, along_cols, along_rows = sets_ref[0, label], sets_ref[1, label], sets_ref[2, label]
        left = STEP * (spread + jnp.maximum(along_cols, 0.0))
        right = STEP * (spread - jnp.minimum(along_cols, 0.0))
        above = STEP * (spread + jnp.maximum(along_rows, 0.0))
        below = STEP * (spread - jnp.minimum(along_rows, 0.0))
        return 1.0 - (left + right + above + below), left, right, above, below

    for k in range(TILES):
        upper, inner, lower = (weights(row, k) for row in strips)
        for w in range(5):
            value = jnp.full((8, TILE), inner[w], jnp.float32)
            coef_ref[k, w] = value
            coef_ref[k, 5 + w] = jnp.where(sub == 0, upper[w], value)
            coef_ref[k, 10 + w] = jnp.where(sub == 7, lower[w], value)


def pair_kernel(class_ref, sets_ref, own_ref, other_ref, u_ref, q_ref, half_ref, columns_ref, coef_ref, *scratch):
    late, early, u, sums_ref, columns, sems = scratch
    strip, core, _, _ = position()
    state = pltpu.make_async_copy(u_ref, u, sems.at[2])

    def both(first, second):
        a = pltpu.make_async_copy(first, late, sems.at[0])
        b = pltpu.make_async_copy(second, early, sems.at[1])
        a.start()
        b.start()
        state.start()
        a.wait()
        b.wait()

    @pl.when(core == 1)
    def _():
        both(own_ref, other_ref)

    @pl.when(core == 0)
    def _():
        both(other_ref, own_ref)

    fill_weights(strip, class_ref, sets_ref, coef_ref)

    def split(value):
        big = value.astype(jnp.bfloat16)
        return big, (value - big.astype(jnp.float32)).astype(jnp.bfloat16)

    def times(a, b):
        return jnp.dot(a, b, preferred_element_type=jnp.float32)

    early_big, early_small = split(early[...])
    for part in range(2):
        rows = slice(part * HALF, (part + 1) * HALF)
        big, small = split(late[rows, :])
        q_ref[rows, :] = times(big, early_big) + (times(big, early_small) + times(small, early_big))
    half_ref[...] = q_ref[pl.ds(pl.multiple_of(core * HALF, HALF), HALF), :]
    cols = pl.ds(pl.multiple_of(strip // 2 * TILE, TILE), TILE)
    wide = jnp.where(core == 1, late[:, cols], q_ref[:, cols])
    turned = jnp.transpose(wide)
    columns[0:LOCAL, :] = jnp.where(lax.rem(strip, 2) == 1, turned[LOCAL:], turned[:LOCAL])
    state.wait()
    for k in range(TILES):
        cols = slice(k * TILE, (k + 1) * TILE)
        for br in range(2):
            part = u[br * BLK : (br + 1) * BLK, cols]
            sums_ref[br * TILES + k : br * TILES + k + 1, :] = jnp.sum(part, axis=0, keepdims=True)
    columns[LOCAL:, :] = jnp.zeros((8, COARSE), jnp.float32)
    columns[LOCAL:, 0:TILE] = jnp.broadcast_to(packed_means(sums_ref[...]), (8, TILE))
    done = pltpu.make_async_copy(columns, columns_ref, sems.at[0])
    done.start()
    done.wait()


def pair_product(tile_class, coeff_sets, own, other, state):
    square = pltpu.VMEM((COARSE, COARSE), jnp.float32)
    return pl.pallas_call(
        pair_kernel,
        cost_estimate=cost(3),
        out_shape=(
            jax.ShapeDtypeStruct((COARSE, COARSE), jnp.float32),
            jax.ShapeDtypeStruct((HALF, COARSE), jnp.float32),
            pltpu.HBM((LOCAL + 8, COARSE), jnp.float32),
            jax.ShapeDtypeStruct((TILES, 15, 8, TILE), jnp.float32),
        ),
        in_specs=[SMEM, SMEM, HBM, ANY, HBM],
        out_specs=(VMEM, VMEM, HBM, VMEM),
        scratch_shapes=[
            square,
            square,
            pltpu.VMEM((ROWS, COLS), jnp.float32),
            pltpu.VMEM((32, TILE), jnp.float32),
            pltpu.VMEM((LOCAL + 8, COARSE), jnp.float32),
            pltpu.SemaphoreType.DMA((3,)),
        ],
        compiler_params=pltpu.CompilerParams(vmem_limit_bytes=24 << 20),
    )(*in_hbm(tile_class, coeff_sets, own), other, *in_hbm(state))


def fine_kernel(corrected, coef, *refs):
    if corrected:
        c_ref, means_ref, own_ref, other_ref, own_columns_ref, columns_ref, *refs = refs
        up_ref, u_ref, down_ref, f_ref, fin_ref, out_ref, *refs = refs
        block, means_scratch, columns_scratch, extra, u_ext, first, second, force, sums_ref, sems = refs
        states, forces = [], []
        for n in range(PARTS):
            tiles = pl.ds(n * TILES // PARTS, TILES // PARTS)
            states.append(pltpu.make_async_copy(u_ref.at[tiles], u_ext.at[tiles, pl.ds(STEPS, ROWS)], sems.at[n]))
            forces.append(pltpu.make_async_copy(f_ref.at[tiles], force.at[tiles], sems.at[PARTS + n]))
        needed = [
            pltpu.make_async_copy(means_ref, means_scratch, extra.at[0]),
            pltpu.make_async_copy(own_columns_ref, columns_scratch, extra.at[1]),
        ]
        for copy in states + forces + needed:
            copy.start()
    else:
        up_ref, u_ref, f_ref, down_ref, fin_ref, out_ref, top_ref, bottom_ref, means_ref, force_ref, *refs = refs
        means_scratch, f_ext, f_sems, u_ext, first, second, force, sums_ref, sems = refs
        copies = []
        for k in range(TILES):
            cols = pl.ds(k * TILE, TILE)
            inner = pl.ds(STEPS, ROWS)
            copies.append(
                (
                    pltpu.make_async_copy(u_ref.at[:, cols], u_ext.at[k, inner], sems.at[k]),
                    pltpu.make_async_copy(f_ref.at[:, cols], f_ext.at[k, inner], f_sems.at[k]),
                )
            )
            for copy in copies[k]:
                copy.start()
    strip, core, _, _ = position()
    sub = iota((8, TILE), 0)
    lane = iota((8, TILE), 1)
    for k in range(TILES):
        cols = slice(k * TILE, (k + 1) * TILE)
        u_ext[k, 0:STEPS, :] = up_ref[0:STEPS, cols]
        u_ext[k, STEPS + ROWS : EXT, :] = down_ref[0:STEPS, cols]
        if not corrected:
            f_ext[k, 0:STEPS, :] = up_ref[STEPS : 2 * STEPS, cols]
            f_ext[k, STEPS + ROWS : EXT, :] = down_ref[STEPS : 2 * STEPS, cols]
    quarter, places = [], []
    if corrected:
        for line in range(4):
            block_row = lax.rem(2 * strip + 15 + line, 16)
            cols = pl.ds(pl.multiple_of(block_row // 4 * TILE, TILE), TILE)
            quarter.append(jnp.broadcast_to(c_ref[:, cols], (8, TILE)))
            places.append(lax.rem(block_row, 4) * 32)
    for k in range(TILES):
        if corrected:
            if k % (TILES // PARTS) == 0:
                states[k * PARTS // TILES].wait()
            added = []
            for line in range(4):
                at = jnp.where(lane < BLK, 2 * k, 2 * k + 1) + places[line]
                added.append(jnp.take_along_axis(quarter[line], at, axis=1))
        else:
            for copy in copies[k]:
                copy.wait()
        for i in range(LINES):
            rows = pl.ds(i * 8, 8)
            value = u_ext[k, pl.ds(i, 8, stride=LINES), :]
            if corrected:
                row = sub * LINES + i
                addend = jnp.where(row < STEPS + BLK, added[1], added[2])
                if i < STEPS:
                    addend = jnp.where(sub == 0, added[0], addend)
                if i >= LINES - STEPS:
                    addend = jnp.where(sub == 7, added[3], addend)
                value = value + addend
            else:
                force[k, rows, :] = STEP * f_ext[k, pl.ds(i, 8, stride=LINES), :]
            first[k, rows, :] = value
    results = []
    if corrected:
        for copy in forces:
            copy.wait()
    else:
        results.append(pltpu.make_async_copy(force, force_ref, f_sems.at[0]))
        results[0].start()

    def tile_step(old, new, k, last=False):
        before = lax.rem(k + TILES - 1, TILES)
        after = lax.rem(k + 1, TILES)
        line = [old[k, pl.ds(i * 8, 8), :] for i in range(LINES)]
        top = pltpu.roll(line[-1], 1, 0)
        bottom = pltpu.roll(line[0], 7, 0)
        for i in range(LINES):
            kind = (i < STEPS) + 2 * (i >= LINES - STEPS)
            centre, w_left, w_right, w_above, w_below = (coef[k, 5 * kind + w] for w in range(5))
            rows = pl.ds(i * 8, 8)
            left = pltpu.roll(jnp.where(lane == TILE - 1, old[before, rows, :], line[i]), 1, 1)
            right = pltpu.roll(jnp.where(lane == 0, old[after, rows, :], line[i]), TILE - 1, 1)
            above = line[i - 1] if i else top
            below = line[i + 1] if i + 1 < LINES else bottom
            new[k, pl.ds(i, 8, stride=LINES) if last else rows, :] = (
                (centre * line[i] + force[k, rows, :])
                + (w_left * left + w_right * right)
                + (w_above * above + w_below * below)
            )

    def sweep(old, new):
        def one_tile(k, carry):
            tile_step(old, new, k)
            return carry

        lax.fori_loop(0, TILES, one_tile, 0, unroll=16)

    def two_steps(_, carry):
        sweep(first, second)
        sweep(second, first)
        return carry

    lax.fori_loop(0, STEPS // 2 - 1, two_steps, 0)
    sweep(first, second)

    def last_tile(k, carry):
        tile_step(second, u_ext, k, last=True)
        for br in range(2):
            part = u_ext[k, STEPS + br * BLK : STEPS + (br + 1) * BLK, :]
            sums_ref[pl.ds(br * TILES + k, 1), :] = jnp.sum(part, axis=0, keepdims=True)
        return carry

    for part in range(4):
        half = TILES // 4
        tiles = pl.ds(part * half, half)
        lax.fori_loop(part * half, (part + 1) * half, last_tile, 0, unroll=4)
        copy = pltpu.make_async_copy(u_ext.at[tiles, pl.ds(STEPS, ROWS)], fin_ref.at[tiles], sems.at[part])
        copy.start()
        results.append(copy)
    if not corrected:
        for k in range(TILES):
            cols = slice(k * TILE, (k + 1) * TILE)
            top_ref[:, cols] = u_ext[k, STEPS : 2 * STEPS, :]
            bottom_ref[:, cols] = u_ext[k, ROWS : STEPS + ROWS, :]
    means = packed_means(sums_ref[...])
    if corrected:
        for copy in needed:
            copy.wait()
        grown = means - means_scratch[...]
        even = core == 0
        pushed = rows_times(grown - jnp.where(even, other_ref[...], 0.0), columns_ref[0:LOCAL, :])
        pushed = pushed - rows_times(jnp.where(even, own_ref[...], 0.0), columns_scratch[0:LOCAL, :])
        write_message(strip, pushed, grown, block, out_ref)
    else:
        out_ref[...] = means
        means_scratch[...] = means
        copy = pltpu.make_async_copy(means_scratch, means_ref, f_sems.at[1])
        copy.start()
        results.append(copy)
    for copy in results:
        copy.wait()


FIELD = pltpu.VMEM((TILES, EXT, TILE), jnp.float32)
EDGE = jax.ShapeDtypeStruct((STEPS, COLS), jnp.float32)


def fine_call(corrected, in_specs, more_out, more_specs, scratch, args):
    return pl.pallas_call(
        functools.partial(fine_kernel, corrected),
        cost_estimate=cost(10),
        out_shape=(pltpu.HBM((TILES, ROWS, TILE), jnp.float32), *more_out),
        in_specs=in_specs,
        out_specs=(HBM, *more_specs),
        scratch_shapes=[
            *scratch,
            FIELD,
            FIELD,
            FIELD,
            FIELD,
            pltpu.VMEM((32, TILE), jnp.float32),
            pltpu.SemaphoreType.DMA((TILES,)),
        ],
        compiler_params=pltpu.CompilerParams(vmem_limit_bytes=16 << 20),
    )(*args)


def first_sweep(coef, upper, state, source, lower):
    state, source = in_hbm(state, source)
    return fine_call(
        False,
        [VMEM, VMEM, HBM, HBM, VMEM],
        (
            jax.ShapeDtypeStruct((1, TILE), jnp.float32),
            EDGE,
            EDGE,
            pltpu.HBM((1, TILE), jnp.float32),
            pltpu.HBM((TILES, EXT, TILE), jnp.float32),
        ),
        (VMEM, VMEM, VMEM, HBM, HBM),
        [pltpu.VMEM((1, TILE), jnp.float32), FIELD, pltpu.SemaphoreType.DMA((TILES,))],
        (coef, upper, state, source, lower),
    )


def second_sweep(coef, correction, means, own_part, other_part, columns, next_columns, state, forcing):
    means, columns, forcing = in_hbm(means, columns, forcing)
    return fine_call(
        True,
        [VMEM, VMEM, HBM, VMEM, VMEM, HBM, VMEM, VMEM, ANY, VMEM, HBM],
        (jax.ShapeDtypeStruct((128 * PIECES, TILE), jnp.float32),),
        (VMEM,),
        [
            pltpu.VMEM((8 * PIECES, TILE), jnp.float32),
            pltpu.VMEM((1, TILE), jnp.float32),
            pltpu.VMEM((LOCAL + 8, COARSE), jnp.float32),
            pltpu.SemaphoreType.DMA((2,)),
        ],
        (coef, correction, means, own_part, other_part, columns, next_columns, *state, forcing),
    )


def rows_times(row, matrix):
    row = jnp.broadcast_to(row, (8, TILE))[:, :LOCAL]
    return jnp.dot(row, matrix, precision=HIGHEST, preferred_element_type=jnp.float32)


def write_message(strip, pushed, raw, block, out_ref):
    lane = iota((1, TILE), 1)
    raw = jnp.where((lane >= LOCAL) == (lax.rem(strip, 2) == 1), raw, 0.0)
    pieces = [pushed[0:1, q * TILE : (q + 1) * TILE] for q in range(4)] + [raw]
    for n in range(8):
        for q in range(PIECES):
            block[n * PIECES + q : n * PIECES + q + 1, :] = pieces[q]
    for n in range(16):
        out_ref[n * 8 * PIECES : (n + 1) * 8 * PIECES, :] = block[...]


def message_kernel(means_ref, base_ref, columns_ref, out_ref, block, out, sem):
    defect = means_ref[...] - base_ref[...]
    strip, _, _, _ = position()
    write_message(strip, rows_times(defect, columns_ref[0:LOCAL, :]), defect, block, out)
    sent = pltpu.make_async_copy(out, out_ref, sem)
    sent.start()
    sent.wait()


def message(means, base, columns):
    return pl.pallas_call(
        message_kernel,
        cost_estimate=cost(1),
        out_shape=pltpu.HBM((128 * PIECES, TILE), jnp.float32),
        in_specs=[VMEM, VMEM, VMEM],
        out_specs=HBM,
        scratch_shapes=[
            pltpu.VMEM((8 * PIECES, TILE), jnp.float32),
            pltpu.VMEM((128 * PIECES, TILE), jnp.float32),
            pltpu.SemaphoreType.DMA,
        ],
        compiler_params=pltpu.CompilerParams(vmem_limit_bytes=16 << 20),
    )(means, base, columns)


def add(a, b):
    return [p + q for p, q in zip(a, b, strict=True)]


def minus(a, b):
    return [p - q for p, q in zip(a, b, strict=True)]


def select(condition, a, b):
    return [jnp.where(condition, p, q) for p, q in zip(a, b, strict=True)]


def quarters(row):
    return [row[:, q * TILE : (q + 1) * TILE] for q in range(4)]


def applied(matrix, vector):
    diagonal = iota((TILE, TILE), 0) == iota((TILE, TILE), 1)
    column = jnp.sum(matrix * jnp.concatenate(vector, axis=1), axis=1, keepdims=True)
    return [
        jnp.sum(jnp.where(diagonal, column[q * TILE : (q + 1) * TILE], 0.0), axis=0, keepdims=True) for q in range(4)
    ]


def pushes(got_ref, window):
    start = lax.rem(window + 16, 16) * (8 * PIECES)
    return [jnp.sum(got_ref[pl.ds(start + q, 8, stride=PIECES), :], axis=0, keepdims=True) for q in range(4)]


def gathered(got_ref, window):
    start = lax.rem(window + 16, 16) * (8 * PIECES) + 4
    raw = got_ref[pl.ds(start, 8, stride=PIECES), :]
    return [raw[2 * q : 2 * q + 1] + raw[2 * q + 1 : 2 * q + 2] for q in range(4)]


def pair_pushes(got_ref, pair):
    at = 2 * lax.rem(pair, 8)
    return add(pushes(got_ref, at - 1), pushes(got_ref, at))


def strip_piece(strip, value):
    piece = value[3]
    for q in range(3):
        piece = jnp.where(strip // 2 == q, value[q], piece)
    return jnp.broadcast_to(piece, (8, TILE))


def first_chain_kernel(got_ref, other_ref, *refs):
    whole, halved = refs[:5], refs[5:11]
    out_ref, maps_ref, maps, sems, out_sems = refs[11:]
    strip, core, chip, y = position()

    def fetch(slot, source):
        for part in range(2):
            rows = pl.ds(part * HALF, HALF)
            pltpu.make_async_copy(source.at[rows], maps.at[slot, rows], sems.at[slot, part]).start()

    def fetch_halves(slot, which):
        for part, at in ((0, core), (1, 1 - core)):
            rows = pl.ds(pl.multiple_of(at * HALF, HALF), HALF)
            pltpu.make_async_copy(halved[2 * which + part], maps.at[slot, rows], sems.at[slot, part]).start()

    def fetch_turned(slot, pair, below):
        own = (core == 0) == below

        @pl.when(own)
        def _():
            fetch(slot, pair[0])

        @pl.when(jnp.logical_not(own))
        def _():
            fetch(slot, pair[1])

    def fetch_near(slot, ahead):
        if ahead == 2:
            fetch_halves(slot, 0)
        else:
            fetch_turned(slot, whole[0:2], ahead == 3)

    def fetch_far(slot, ahead):
        if ahead in (0, 2):
            fetch_halves(slot, 2 if ahead else 1)
        else:
            fetch_turned(slot, whole[2:4], ahead == 3)

    def landed(slot):
        for part in range(2):
            rows = pl.ds(0, HALF)
            pltpu.make_async_copy(whole[4].at[rows], maps.at[slot, rows], sems.at[slot, part]).wait()
        kept(slot).start()

    def kept(slot):
        return pltpu.make_async_copy(maps.at[slot], maps_ref.at[slot], out_sems.at[slot])

    for half in range(2):
        if half == 1:
            fetch_far(4, 0)
        for ahead in range(1, 4):
            wraps = y + ahead >= 4

            @pl.when(wraps == (half == 0))
            def _():
                fetch_far(4 * half + ahead, ahead)

            @pl.when(wraps != (half == 0))
            def _():
                fetch_near(4 * half + ahead, ahead)

    fetch(0, whole[4])
    fetch(8, other_ref)
    value = select(core == 1, pushes(got_ref, 2 * chip), pair_pushes(got_ref, chip))

    def arriving(step, value):
        landed(step)
        return add(applied(maps[step], value), pair_pushes(got_ref, chip + step))

    value = lax.fori_loop(1, 8, arriving, value)
    landed(0)
    landed(8)

    def again(step, value):
        return add(applied(maps[step], value), pair_pushes(got_ref, chip + step))

    value = lax.fori_loop(0, 8, again, value)
    value = select(core == 1, applied(maps[8], add(value, gathered(got_ref, 2 * chip + 15))), value)
    piece = strip_piece(strip, value)
    lane = iota((8, TILE), 1)
    here = jnp.where((lane < LOCAL) == (lax.rem(strip, 2) == 0), piece, pltpu.roll(piece, LOCAL, 1))
    out_ref[...] = jnp.concatenate(value + [here[0:1]], axis=1)
    for slot in range(9):
        kept(slot).wait()


def first_chain(got, other, whole, halved):
    whole[4], halved[2] = in_hbm(whole[4], halved[2])
    return pl.pallas_call(
        first_chain_kernel,
        cost_estimate=cost(5),
        out_shape=(
            jax.ShapeDtypeStruct((1, COARSE + TILE), jnp.float32),
            pltpu.HBM((9, COARSE, COARSE), jnp.float32),
        ),
        in_specs=[VMEM] + [ANY] * 12,
        out_specs=(VMEM, HBM),
        scratch_shapes=[
            pltpu.VMEM((9, COARSE, COARSE), jnp.float32),
            pltpu.SemaphoreType.DMA((9, 2)),
            pltpu.SemaphoreType.DMA((9,)),
        ],
        compiler_params=pltpu.CompilerParams(vmem_limit_bytes=16 << 20),
    )(got, other, *whole, *halved)


def last_chain_kernel(got_ref, partner_ref, maps_ref, u_ref, out_ref, maps, sems, u, whole, sem, out_sems):
    strip, core, chip, _ = position()

    def fetched(slot):
        return pltpu.make_async_copy(maps_ref.at[slot], maps.at[slot], sems.at[slot])

    for slot in (0, 1, 2, 3, 4, 5, 6, 7, 8):
        fetched(slot).start()
    state = pltpu.make_async_copy(u_ref, u, sem)
    state.start()
    partner = quarters(partner_ref[...])
    even_start, odd_pushes = pair_pushes(got_ref, chip), pushes(got_ref, 2 * chip)
    fetched(0).wait()
    value = select(core == 1, add(odd_pushes, applied(maps[0], partner)), even_start)

    def arriving(step, value):
        fetched(step).wait()
        return add(applied(maps[step], value), pair_pushes(got_ref, chip + step))

    value = lax.fori_loop(1, 8, arriving, value)

    def again(step, value):
        return add(applied(maps[step], value), pair_pushes(got_ref, chip + step))

    value = lax.fori_loop(0, 8, again, value)
    fetched(8).wait()
    final = applied(maps[8], add(value, minus(gathered(got_ref, 2 * chip + 15), partner)))
    piece = strip_piece(strip, select(core == 1, final, value))
    state.wait()
    lane = iota((8, TILE), 1)
    outs = []
    for k in range(TILES):
        cols = slice(k * TILE, (k + 1) * TILE)
        for br in range(2):
            at = lax.rem(strip, 2) * LOCAL + br * 32 + 2 * k
            added = jnp.take_along_axis(piece, at + jnp.where(lane < BLK, 0, 1), axis=1)
            for n in range(BLK // 8):
                rows = slice(br * BLK + n * 8, br * BLK + (n + 1) * 8)
                whole[rows, cols] = u[k, rows, :] + added
        if k % 4 == 3:
            cols = pl.ds((k - 3) * TILE, 4 * TILE)
            copy = pltpu.make_async_copy(whole.at[:, cols], out_ref.at[:, cols], out_sems.at[k // 4])
            copy.start()
            outs.append(copy)
    for copy in outs:
        copy.wait()


def last_chain(got, partner, maps, previous):
    return pl.pallas_call(
        last_chain_kernel,
        cost_estimate=cost(6),
        out_shape=jax.ShapeDtypeStruct((ROWS, COLS), jnp.float32),
        in_specs=[VMEM, VMEM, HBM, ANY],
        out_specs=HBM,
        scratch_shapes=[
            pltpu.VMEM((9, COARSE, COARSE), jnp.float32),
            pltpu.SemaphoreType.DMA((9,)),
            pltpu.VMEM((TILES, ROWS, TILE), jnp.float32),
            pltpu.VMEM((ROWS, COLS), jnp.float32),
            pltpu.SemaphoreType.DMA,
            pltpu.SemaphoreType.DMA((4,)),
        ],
        compiler_params=pltpu.CompilerParams(vmem_limit_bytes=16 << 20),
    )(got, partner, *in_hbm(maps), previous)


def exchanged(block):
    block = block.reshape(128, 1, PIECES * TILE)
    return lax.all_to_all(block, ("tm", "space"), 0, 0, tiled=True).reshape(128 * PIECES, TILE)


def swapped(value):
    return moved(value, lambda x, y, z, core: (x, y, z, 1 - core))


def across(value):
    return moved(value, lambda x, y, z, core: (x, y, z + 1 - 2 * core, core))


def along(value, dz=0):
    return moved(value, lambda x, y, z, core: (x, y + 1 - 2 * core, z + dz * (1 - 2 * core), core))


def per_device(initial_states, sources, tile_class, coeff_sets, coarse_maps):
    state, source, own_map = initial_states[0], sources[0], coarse_maps[0]
    core = lax.axis_index("tm") % 2
    other_map = swapped(own_map)
    upper = shifted(jnp.concatenate([state[-STEPS:], source[-STEPS:]], axis=0), 0, 1)
    lower = shifted(jnp.concatenate([state[:STEPS], source[:STEPS]], axis=0), 0, -1)

    product, half, columns, coef = pair_product(tile_class, coeff_sets, own_map, other_map, state)
    product, half, columns, upper, lower = lax.optimization_barrier((product, half, columns, upper, lower))
    near = along(product)
    far_same = across(half)
    next_columns = shifted(columns, -1)

    finished, means, top, bottom, kept_means, forcing = first_sweep(coef, upper, state, source, lower)
    block = message(means, next_columns[LOCAL : LOCAL + 1, :TILE], next_columns)
    near, far_same, next_columns, block, finished = lax.optimization_barrier(
        (near, far_same, next_columns, block, finished)
    )
    near_half = lax.dynamic_slice(near, (core * HALF, 0), (HALF, COARSE))
    far = across(near)
    near_second = along(near_half)
    far_second = along(near_half, 1)

    got = exchanged(block)

    got, far, near_second, far_second, finished, top, bottom = lax.optimization_barrier(
        (got, far, near_second, far_second, finished, top, bottom)
    )
    previous = shifted(bottom, 1, 1), shifted(finished, 1), shifted(top, 1, -1)
    whole = [near, swapped(near), far, swapped(far), product]
    halved = []
    for part in (near_second, far_same, far_second):
        halved += [part, swapped(part)]
    correction, maps = first_chain(got, other_map, whole, halved)
    partner = swapped(correction)
    here, there = correction[:, :COARSE], partner[:, :COARSE]
    own_part, other_part = correction[:, COARSE:], partner[:, COARSE:]

    finished, block = second_sweep(
        coef, here, kept_means, own_part, other_part, columns, next_columns, previous, forcing
    )
    previous = shifted(finished, 1)
    got = exchanged(block)
    return last_chain(got, there, maps, previous)[None]


def solution(mesh):
    placed = (P("tm", "space", None), P("tm", "space", None), P(), P(), P("tm", None, None))
    return jax.shard_map(
        per_device, mesh=mesh, in_specs=placed, out_specs=P("tm", "space", None), check_vma=False
    )
```
